512 devices in a mesh: seq: 32 (over x, z_lo), head: 8 (over y, core), enc: 2 (over z_hi).
Axes of the slice: x: 4, y: 4, z: 16 (z_hi: 2, z_lo: 8; z = z_hi * 8 + z_lo), core: 2. Of those that a mesh axis runs over, the one named last changes fastest.
Arguments:
- queries: bfloat16 [10240, 4096], P('seq', ('head', 'enc')), may hold values from -2000 to 2000
- keys: bfloat16 [10240, 4096], P('seq', ('head', 'enc')), may hold values from -2000 to 2000
- values: bfloat16 [10240, 4096], P('seq', ('head', 'enc')), may hold values from -6 to 6
- out_weight: bfloat16 [4096, 5120], P(('head', 'enc'), 'seq'), may hold values from -0.1875 to 0.1875
- q_gain: float32 [4096], P(('head', 'enc')), may hold values from 0.75 to 3
- k_gain: float32 [4096], P(('head', 'enc')), may hold values from 0.75 to 3
- gate: float32 [5120], P(('head', 'enc')), may hold values from 1 to 8
- valid_count: int32 [1], replicated, may hold values from 5120 to 10240
Outputs:
- update: bfloat16 [10240, 5120], P('seq', ('head', 'enc'))
The draws below stay inside these ranges and needn't reach their ends.
Inputs may be any that keep to these rules, and one draw needn't show every extreme that they name: Key positions from valid_count[0] on are padding and take no weight.
All inputs are finite; a program needn't handle non-finite values.
Results may differ from the reference program's by a relative error of at most 0.015.
The reference program's roundings to bfloat16 on the way count: a program that leaves them out, or rounds other values in their place, can miss the bound.
Values may be sent and summed in bfloat16 or wider, within the bound.
No kernel may reach another device: no remote copies, remote signals or barrier semaphores. Data moves between devices by JAX's collectives and lax.ppermute only.
A program may use at most 64 MiB of HBM per device.

```python
import math
import jax
import jax.numpy as jnp
from jax import lax

D = 5120
HEAD_DIM = 128
GROUPS = 16
HEADS = 32
FEATURES = 4096
SEQ_LEN = 10240


def joint_draw(key):
    folded = jax.random.fold_in(key, 4111)
    subkeys = jax.random.split(folded, 5)
    column_head = jnp.arange(FEATURES) // HEAD_DIM
    rising = 1.0 + 2.0 * column_head.astype(jnp.float32) / max(HEADS - 1, 1)
    column_scale = rising * jnp.exp(jax.random.uniform(subkeys[0], (FEATURES,), minval=0.0, maxval=jnp.log(3.0)))
    row_query = jnp.exp(jax.random.uniform(subkeys[1], (SEQ_LEN, 1), minval=0.0, maxval=jnp.log(10.0)))
    row_key = jnp.exp(jax.random.uniform(subkeys[2], (SEQ_LEN, 1), minval=0.0, maxval=jnp.log(10.0)))
    query_draw = jax.random.normal(subkeys[3], (SEQ_LEN, FEATURES)) * row_query * column_scale[None, :]
    key_draw = jax.random.normal(subkeys[4], (SEQ_LEN, FEATURES)) * row_key * column_scale[None, :]
    query_draw = jnp.clip(query_draw, -2000.0, 2000.0)
    key_draw = jnp.clip(key_draw, -2000.0, 2000.0)
    return (query_draw.astype(jnp.bfloat16), key_draw.astype(jnp.bfloat16))


def draw_queries(key, part):
    return joint_draw(key)[0]


def draw_keys(key, part):
    return joint_draw(key)[1]


def spiked(drawn, stream_key, source, target, parts, factor):
    owner, partner = [(jnp.arange(drawn.shape[position]) // (drawn.shape[position] // parts)).reshape([-1 if axis == position else 1 for axis in range(drawn.ndim)]) for position in (source, target)]
    chosen = jax.random.permutation(stream_key, parts)[partner]
    strong = (owner == chosen) | (owner == (partner + parts // 2) % parts)
    return jnp.where(strong, factor * drawn, drawn)


def steps_of(key, shape, cuts, smallest, top_value):
    gain, own = 1.0, jax.random.fold_in(key, 6)
    for position, parts in cuts:
        heights = jnp.exp(jax.random.uniform(jax.random.fold_in(own, position), (parts,), jnp.float32, smallest / len(cuts), top_value / len(cuts)))
        gain = gain * jnp.repeat(heights, shape[position] // parts).reshape([-1 if axis == position else 1 for axis in range(len(shape))])
    return gain


def normal_values(stream_key, dims, scale, most, pieces=(), kind=jnp.bfloat16):
    result = scale * jax.random.normal(stream_key, dims, jnp.float32)
    if pieces:
        result = result * steps_of(stream_key, dims, pieces, -0.22, 0.18)
    return jnp.clip(result, -most, most).astype(kind)


def bell_draw_with(stream_key, extent, width, bound, pieces, heavy, kind=jnp.bfloat16):
    drawn = width * jax.random.normal(stream_key, extent, jnp.float32)
    if pieces:
        drawn = drawn * steps_of(stream_key, extent, pieces, -0.22, 0.18)
    return jnp.clip(spiked(drawn, jax.random.fold_in(stream_key, 3), *heavy), -bound, bound).astype(kind)


def setup_inputs(seed: int = 0) -> dict:
    key_list = jax.random.split(jax.random.key(seed), 9)
    queries = draw_queries(jax.random.fold_in(key_list[8], 71), 0)
    keys = draw_keys(jax.random.fold_in(key_list[8], 71), 0)
    values = normal_values(key_list[2], (SEQ_LEN, FEATURES), 1.0, 6.0, ((0, 32), (1, 16)))
    out_weight = bell_draw_with(key_list[3], (FEATURES, D), FEATURES ** -0.5, 0.1875, ((0, 16), (1, 32)), (0, 1, 32, 2.75))
    q_gain = jnp.clip(jnp.exp(math.log(3.0) - 1.3862944 * jax.random.uniform(key_list[4], (FEATURES,), jnp.float32) ** steps_of(key_list[4], (FEATURES,), ((0, 16),), -0.2, 0.2)), 0.75, 3.0)
    k_gain = jnp.clip(jnp.exp(math.log(3.0) - 1.3862944 * jax.random.uniform(key_list[5], (FEATURES,), jnp.float32) ** steps_of(key_list[5], (FEATURES,), ((0, 16),), -0.2, 0.2)), 0.75, 3.0)
    gate = jnp.clip(jnp.exp(math.log(8.0) - 2.0794415 * jax.random.uniform(key_list[6], (D,), jnp.float32) ** steps_of(key_list[6], (D,), ((0, 16),), -0.2, 0.2)), 1.0, 8.0)
    valid_count = jax.random.randint(key_list[7], (1,), SEQ_LEN // 2, SEQ_LEN + 1).astype(jnp.int32)
    return {"queries": queries, "keys": keys, "values": values, "out_weight": out_weight, "q_gain": q_gain, "k_gain": k_gain, "gate": gate, "valid_count": valid_count}


epsilon = 1e-06

def normalize(matrix, gain_row):
    values32 = matrix.astype(jnp.float32)
    mean_square = lax.optimization_barrier(jnp.mean(values32 * values32, axis=1, keepdims=True))
    return (values32 * lax.rsqrt(mean_square + epsilon) * gain_row[None, :]).astype(jnp.bfloat16)

def reference(queries, keys, values, out_weight, q_gain, k_gain, gate, valid_count):
    query_norm = normalize(queries, q_gain)
    key_norm = normalize(keys, k_gain)
    key_limit = valid_count[0]
    usable = jnp.arange(SEQ_LEN, dtype=jnp.int32) < key_limit
    score_scale = HEAD_DIM ** (-0.5)
    block_size = 512 if SEQ_LEN % 512 == 0 else SEQ_LEN

    def split_heads(matrix):
        return matrix.reshape(SEQ_LEN, HEADS, HEAD_DIM).transpose(1, 0, 2)

    def attend_head(triple):
        query_head, key_head, value_head = triple
        query_blocks = query_head.reshape(SEQ_LEN // block_size, block_size, HEAD_DIM)

        def attend_block(query_block):
            scores = jnp.dot(query_block, jnp.transpose(key_head), preferred_element_type=jnp.float32) * score_scale
            scores = jnp.where(usable[None, :], scores, -jnp.inf)
            row_max = lax.optimization_barrier(jnp.max(scores, axis=1, keepdims=True))
            weights = jnp.exp(scores - row_max)
            numerator = jnp.dot(weights.astype(jnp.bfloat16), value_head, preferred_element_type=jnp.float32)
            return numerator / lax.optimization_barrier(jnp.sum(weights, axis=1, keepdims=True))
        return lax.map(attend_block, query_blocks).reshape(SEQ_LEN, HEAD_DIM)
    head_outputs = lax.map(attend_head, (split_heads(query_norm), split_heads(key_norm), split_heads(values)))
    attended = head_outputs.transpose(1, 0, 2).reshape(SEQ_LEN, FEATURES).astype(jnp.bfloat16)
    group_width = FEATURES // GROUPS
    attended_groups = attended.reshape(SEQ_LEN, GROUPS, group_width).transpose(1, 0, 2)
    weight_groups = out_weight.reshape(GROUPS, group_width, D)

    def add_group(running, pair):
        group_rows, group_weight = pair
        partial_sum = jnp.dot(group_rows, group_weight, preferred_element_type=jnp.float32).astype(jnp.bfloat16)
        partial_sum = lax.optimization_barrier(partial_sum)
        return (running + partial_sum.astype(jnp.float32), None)
    projected, _ = lax.scan(add_group, jnp.zeros((SEQ_LEN, D), jnp.float32), (attended_groups, weight_groups))
    return (gate[None, :] * projected).astype(jnp.bfloat16)
```

```python
import functools
import math

import jax
import jax.numpy as jnp
from jax import lax
from jax.experimental import pallas as pl
from jax.experimental.pallas import tpu as pltpu
from jax.sharding import Mesh
from jax.sharding import PartitionSpec as P

HEAD_DIM = 128
EPSILON = 1e-06
BIAS = -1e30
F32 = jnp.float32
BF16 = jnp.bfloat16
AXES = ("x", "zl", "y", "core", "zh")
SIZES = (4, 8, 4, 2, 2)
SWAP = ((0, 1), (1, 0))


def attention_kernel(
    limit_ref, q_ref, kv_ref, inverse_ref, gain_ref, out_ref, kt_ref, ve_ref, *, heads, keys
):
    tile = q_ref.shape[0]
    factor = HEAD_DIM**-0.5 * math.log2(math.e)

    @pl.when(pl.program_id(0) == 0)
    def _():
        position = lax.broadcasted_iota(jnp.int32, (HEAD_DIM, keys), 1)
        row = lax.broadcasted_iota(jnp.int32, (HEAD_DIM, keys), 0)
        bias = jnp.where((position >= limit_ref[0]) & (row == 0), BIAS, 0.0).astype(BF16)
        for h in range(heads):
            columns = slice(h * HEAD_DIM, (h + 1) * HEAD_DIM)
            raw = kv_ref[:, columns].T.astype(F32)
            kt_ref[h, :HEAD_DIM, :] = (raw * inverse_ref[...] * gain_ref[columns, :]).astype(BF16)
            kt_ref[h, HEAD_DIM:, :] = bias
            ve_ref[h, :, :HEAD_DIM] = kv_ref[:, (heads + h) * HEAD_DIM : (heads + h + 1) * HEAD_DIM]
            ve_ref[h, :, HEAD_DIM:] = jnp.ones((keys, HEAD_DIM), BF16)

    lane = lax.broadcasted_iota(jnp.int32, (tile, HEAD_DIM), 1)
    first = jnp.where(lane == 0, 1.0, 0.0).astype(BF16)
    stats = jnp.zeros((tile, HEAD_DIM), F32)
    for h in range(heads):
        query = jnp.concatenate([q_ref[:, h * HEAD_DIM : (h + 1) * HEAD_DIM], first], axis=1)
        scores = jnp.dot(query, kt_ref[h], preferred_element_type=F32)
        top = (jnp.max(scores, axis=1, keepdims=True) * factor).astype(BF16).astype(F32)
        weights = jnp.exp2(scores * factor - top).astype(BF16)
        summed = jnp.dot(weights, ve_ref[h], preferred_element_type=F32)
        out_ref[:, h * HEAD_DIM : (h + 1) * HEAD_DIM] = summed[:, :HEAD_DIM].astype(BF16)
        mass = summed[:, HEAD_DIM:]
        high = mass.astype(BF16).astype(F32)
        stats = jnp.where(lane == 3 * h, top, stats)
        stats = jnp.where(lane == 3 * h + 1, high, stats)
        stats = jnp.where(lane == 3 * h + 2, mass - high, stats)
    out_ref[:, heads * HEAD_DIM :] = stats.astype(BF16)


def attention(limit, queries, keys_values, inverse, gain):
    rows, width = queries.shape
    keys = keys_values.shape[0]
    heads = width // HEAD_DIM
    tile = 256
    return pl.pallas_call(
        functools.partial(attention_kernel, heads=heads, keys=keys),
        grid=(rows // tile,),
        in_specs=[
            pl.BlockSpec(memory_space=pltpu.SMEM),
            pl.BlockSpec((tile, width), lambda i: (i, 0)),
            pl.BlockSpec((keys, 2 * width), lambda i: (0, 0)),
            pl.BlockSpec((1, keys), lambda i: (0, 0)),
            pl.BlockSpec((width, 1), lambda i: (0, 0)),
        ],
        out_specs=pl.BlockSpec((tile, width + HEAD_DIM), lambda i: (i, 0)),
        out_shape=jax.ShapeDtypeStruct((rows, width + HEAD_DIM), BF16),
        scratch_shapes=[
            pltpu.VMEM((heads, 2 * HEAD_DIM, keys), BF16),
            pltpu.VMEM((heads, keys, 2 * HEAD_DIM), BF16),
        ],
        compiler_params=pltpu.CompilerParams(vmem_limit_bytes=48 << 20),
        cost_estimate=pl.CostEstimate(
            flops=8 * rows * keys * width, bytes_accessed=4 << 20, transcendentals=rows * keys * heads
        ),
    )(limit, queries, keys_values, inverse, gain)


def join_kernel(parts_ref, out_ref, *, heads):
    count = parts_ref.shape[0]
    base = heads * HEAD_DIM
    for h in range(heads):
        tops = [parts_ref[i, :, base + 3 * h : base + 3 * h + 1].astype(F32) for i in range(count)]
        highest = functools.reduce(jnp.maximum, tops)
        total = jnp.zeros(out_ref.shape[:1] + (HEAD_DIM,), F32)
        mass = jnp.zeros_like(highest)
        for i in range(count):
            share = jnp.exp2(tops[i] - highest)
            part = parts_ref[i, :, base + 3 * h + 1 : base + 3 * h + 2].astype(F32)
            part = part + parts_ref[i, :, base + 3 * h + 2 : base + 3 * h + 3].astype(F32)
            mass = mass + share * part
            total = total + share * parts_ref[i, :, h * HEAD_DIM : (h + 1) * HEAD_DIM].astype(F32)
        out_ref[:, h * HEAD_DIM : (h + 1) * HEAD_DIM] = (total * (1.0 / mass)).astype(BF16)


def join(parts, width):
    return pl.pallas_call(
        functools.partial(join_kernel, heads=width // HEAD_DIM),
        out_shape=jax.ShapeDtypeStruct((parts.shape[1], width), BF16),
        compiler_params=pltpu.CompilerParams(vmem_limit_bytes=32 << 20),
    )(parts)


def project_kernel(place_ref, own_ref, zh_ref, core_ref, both_ref, weight_ref, out_ref):
    rows = out_ref.shape[1]
    core, zh = place_ref[0], place_ref[1]
    for r in range(2):
        total = jnp.zeros((rows, weight_ref.shape[2]), F32)
        for ref, a, b in (
            (own_ref, core, zh),
            (zh_ref, core, 1 - zh),
            (core_ref, 1 - core, zh),
            (both_ref, 1 - core, 1 - zh),
        ):
            block = weight_ref[a * 4 + b * 2 + r, 0]
            total = total + lax.dot_general(
                ref[...], block, (((1,), (1,)), ((), ())), preferred_element_type=F32
            )
        out_ref[0, :, r * weight_ref.shape[2] : (r + 1) * weight_ref.shape[2]] = total.astype(BF16)


def project(place, pieces, weights):
    rows, width = pieces[0].shape
    blocks, groups, columns, _ = weights.shape
    whole = pl.BlockSpec((rows, width), lambda i: (0, 0))
    return pl.pallas_call(
        project_kernel,
        grid=(groups,),
        in_specs=[pl.BlockSpec(memory_space=pltpu.SMEM)]
        + [whole] * 4
        + [pl.BlockSpec((blocks, 1, columns, width), lambda i: (0, i, 0, 0))],
        out_specs=pl.BlockSpec((1, rows, 2 * columns), lambda i: (i, 0, 0)),
        out_shape=jax.ShapeDtypeStruct((groups, rows, 2 * columns), BF16),
        compiler_params=pltpu.CompilerParams(vmem_limit_bytes=32 << 20),
    )(place, *pieces, weights)


def weight_routes():
    routes = []
    for zl in range(8):
        c, z, r = zl // 4, zl // 2 % 2, zl % 2
        for a in range(2):
            for b in range(2):
                routes.append(((zl * 2 + a) * 2 + b, ((a * 4 + b * 2 + r) * 2 + c) * 2 + z))
    return routes


def local(queries, keys, values, out_weight, q_gain, k_gain, gate, valid_count):
    rows, width = queries.shape
    features = width * 16
    gathered = lax.all_gather(jnp.concatenate([keys, values], axis=1), "zl", axis=0, tiled=True)
    weights = lax.ppermute(out_weight.T, ("zl", "core", "zh"), weight_routes())

    squares = jnp.stack(
        [
            jnp.sum(jnp.square(queries.astype(F32)), axis=1),
            jnp.sum(jnp.square(keys.astype(F32)), axis=1),
        ]
    )
    near = lax.all_to_all(
        jnp.broadcast_to(squares[None], (8, 2, rows)), ("y", "core"), 0, 0, tiled=True
    )
    near = jnp.sum(near, axis=0)
    spread = lax.all_to_all(
        jnp.broadcast_to(near[None], (16, 2, rows)), ("zl", "zh"), 0, 0, tiled=True
    )
    totals = jnp.sum(spread.reshape(8, 2, 2, rows), axis=1)
    inverse = lax.rsqrt(totals / features + EPSILON)
    key_inverse = inverse[:, 1].reshape(1, 8 * rows)
    query_inverse = lax.dynamic_index_in_dim(inverse, lax.axis_index("zl"), keepdims=False)[0]
    query_norm = (queries.astype(F32) * query_inverse[:, None] * q_gain[None, :]).astype(BF16)
    query_all = lax.all_gather(query_norm, "x", axis=0, tiled=True)
    weights = lax.all_gather(weights, "x", axis=0, tiled=False)
    weights = lax.all_gather(weights, "zl", axis=0, tiled=False)

    limit = valid_count - lax.axis_index("x") * (8 * rows)
    parts = attention(limit, query_all, gathered, key_inverse, k_gain[:, None])
    parts = lax.all_to_all(parts.reshape(4, rows, width + HEAD_DIM), "x", 0, 0, tiled=True)
    own = join(parts, width)
    across = lax.ppermute(own, "zh", SWAP)
    beside = lax.ppermute(own, "core", SWAP)
    both = lax.ppermute(across, "core", SWAP)
    place = jnp.stack([lax.axis_index("core"), lax.axis_index("zh")]).astype(jnp.int32)
    terms = project(place, (own, across, beside, both), weights)
    terms = lax.all_to_all(terms, "y", 0, 0, tiled=True)
    summed = jnp.sum(terms.astype(F32), axis=0)
    return (gate[None, :] * summed).astype(BF16)


def solution(mesh):
    fine = Mesh(mesh.devices.reshape(SIZES), AXES)
    tokens, features = ("x", "zl"), ("y", "core", "zh")
    placed = (
        P(tokens, features),
        P(tokens, features),
        P(tokens, features),
        P(features, tokens),
        P(features),
        P(features),
        P(features),
        P(),
    )
    return jax.shard_map(
        local, mesh=fine, in_specs=placed, out_specs=P(tokens, features), check_vma=False
    )
```

```python
import functools
import math

import jax
import jax.numpy as jnp
import numpy as np
from jax import lax
from jax.experimental import pallas as pl
from jax.experimental.pallas import tpu as pltpu
from jax.sharding import Mesh
from jax.sharding import PartitionSpec as P

HEAD_DIM = 128
EPSILON = 1e-06
BIAS = -1e30
F32 = jnp.float32
BF16 = jnp.bfloat16
AXES = ("x", "zl", "y", "core", "zh")
SIZES = (4, 8, 4, 2, 2)
SWAP = ((0, 1), (1, 0))
RING = [0, 2, 4, 6, 7, 5, 3, 1]


def attention_kernel(
    q_ref, kv_ref, inverse_ref, bias_ref, gain_ref, out_ref, kt_ref, ve_ref, *, heads, keys
):
    tile = q_ref.shape[1]
    factor = HEAD_DIM**-0.5 * math.log2(math.e)

    @pl.when(pl.program_id(0) == 0)
    def _():
        row = lax.broadcasted_iota(jnp.int32, (HEAD_DIM, keys), 0)
        bias = jnp.where(row == 0, bias_ref[...], 0.0).astype(BF16)
        for h in range(heads):
            columns = slice(h * HEAD_DIM, (h + 1) * HEAD_DIM)
            raw = kv_ref[:, columns].T.astype(F32)
            kt_ref[h, :HEAD_DIM, :] = (raw * inverse_ref[...] * gain_ref[columns, :]).astype(BF16)
            kt_ref[h, HEAD_DIM:, :] = bias
            ve_ref[h, :, :HEAD_DIM] = kv_ref[:, (heads + h) * HEAD_DIM : (heads + h + 1) * HEAD_DIM]
            ve_ref[h, :, HEAD_DIM:] = jnp.ones((keys, HEAD_DIM), BF16)

    lane = lax.broadcasted_iota(jnp.int32, (tile, HEAD_DIM), 1)
    first = jnp.where(lane == 0, 1.0, 0.0).astype(BF16)
    stats = jnp.zeros((tile, HEAD_DIM), F32)
    for h in range(heads):
        query = jnp.concatenate([q_ref[0, :, h * HEAD_DIM : (h + 1) * HEAD_DIM], first], axis=1)
        scores = jnp.dot(query, kt_ref[h], preferred_element_type=F32)
        top = (jnp.max(scores, axis=1, keepdims=True) * factor).astype(BF16).astype(F32)
        weights = jnp.exp2(scores * factor - top).astype(BF16)
        summed = jnp.dot(weights, ve_ref[h], preferred_element_type=F32)
        out_ref[0, :, h * HEAD_DIM : (h + 1) * HEAD_DIM] = summed[:, :HEAD_DIM].astype(BF16)
        mass = summed[:, HEAD_DIM:]
        high = mass.astype(BF16).astype(F32)
        stats = jnp.where(lane == 3 * h, top, stats)
        stats = jnp.where(lane == 3 * h + 1, high, stats)
        stats = jnp.where(lane == 3 * h + 2, mass - high, stats)
    out_ref[0, :, heads * HEAD_DIM :] = stats.astype(BF16)


def attention(queries, keys_values, inverse, bias, gain, rows):
    blocks, _, width = queries.shape
    keys = keys_values.shape[0]
    heads = width // HEAD_DIM
    return pl.pallas_call(
        functools.partial(attention_kernel, heads=heads, keys=keys),
        grid=(blocks,),
        in_specs=[
            pl.BlockSpec((1, rows, width), lambda i: (i, 0, 0)),
            pl.BlockSpec((keys, 2 * width), lambda i: (0, 0)),
            pl.BlockSpec((1, keys), lambda i: (0, 0)),
            pl.BlockSpec((1, keys), lambda i: (0, 0)),
            pl.BlockSpec((width, 1), lambda i: (0, 0)),
        ],
        out_specs=pl.BlockSpec((1, rows, width + HEAD_DIM), lambda i: (i, 0, 0)),
        out_shape=jax.ShapeDtypeStruct((blocks, rows, width + HEAD_DIM), BF16),
        scratch_shapes=[
            pltpu.VMEM((heads, 2 * HEAD_DIM, keys), BF16),
            pltpu.VMEM((heads, keys, 2 * HEAD_DIM), BF16),
        ],
        compiler_params=pltpu.CompilerParams(vmem_limit_bytes=48 << 20),
        cost_estimate=pl.CostEstimate(
            flops=8 * blocks * rows * keys * width,
            bytes_accessed=4 << 20,
            transcendentals=blocks * rows * keys * heads,
        ),
    )(queries, keys_values, inverse, bias, gain)


def join_kernel(parts_ref, out_ref, *, heads):
    count = parts_ref.shape[0]
    base = heads * HEAD_DIM
    for h in range(heads):
        tops = [parts_ref[i, :, base + 3 * h : base + 3 * h + 1].astype(F32) for i in range(count)]
        highest = functools.reduce(jnp.maximum, tops)
        total = jnp.zeros(out_ref.shape[:1] + (HEAD_DIM,), F32)
        mass = jnp.zeros_like(highest)
        for i in range(count):
            share = jnp.exp2(tops[i] - highest)
            part = parts_ref[i, :, base + 3 * h + 1 : base + 3 * h + 2].astype(F32)
            part = part + parts_ref[i, :, base + 3 * h + 2 : base + 3 * h + 3].astype(F32)
            mass = mass + share * part
            total = total + share * parts_ref[i, :, h * HEAD_DIM : (h + 1) * HEAD_DIM].astype(F32)
        out_ref[:, h * HEAD_DIM : (h + 1) * HEAD_DIM] = (total * (1.0 / mass)).astype(BF16)


def join(parts, width):
    return pl.pallas_call(
        functools.partial(join_kernel, heads=width // HEAD_DIM),
        out_shape=jax.ShapeDtypeStruct((parts.shape[1], width), BF16),
        compiler_params=pltpu.CompilerParams(vmem_limit_bytes=32 << 20),
    )(parts)


def project_kernel(place_ref, own_ref, zh_ref, core_ref, both_ref, weight_ref, out_ref):
    rows = out_ref.shape[1]
    core, zh = place_ref[0], place_ref[1]
    for r in range(2):
        total = jnp.zeros((rows, weight_ref.shape[2]), F32)
        for ref, a, b in (
            (own_ref, core, zh),
            (zh_ref, core, 1 - zh),
            (core_ref, 1 - core, zh),
            (both_ref, 1 - core, 1 - zh),
        ):
            pair = a * 2 + b
            block = weight_ref[pair if r == 0 else 7 - pair, 0]
            total = total + lax.dot_general(
                ref[...], block, (((1,), (1,)), ((), ())), preferred_element_type=F32
            )
        out_ref[0, :, r * weight_ref.shape[2] : (r + 1) * weight_ref.shape[2]] = total.astype(BF16)


def project(place, pieces, weights):
    rows, width = pieces[0].shape
    blocks, groups, columns, _ = weights.shape
    whole = pl.BlockSpec((rows, width), lambda i: (0, 0))
    return pl.pallas_call(
        project_kernel,
        grid=(groups,),
        in_specs=[pl.BlockSpec(memory_space=pltpu.SMEM)]
        + [whole] * 4
        + [pl.BlockSpec((blocks, 1, columns, width), lambda i: (0, i, 0, 0))],
        out_specs=pl.BlockSpec((1, rows, 2 * columns), lambda i: (i, 0, 0)),
        out_shape=jax.ShapeDtypeStruct((groups, rows, 2 * columns), BF16),
        compiler_params=pltpu.CompilerParams(vmem_limit_bytes=32 << 20),
    )(place, *pieces, weights)


def weight_routes():
    routes = []
    for zl in range(8):
        c, z, r = zl // 4, zl // 2 % 2, zl % 2
        for a in range(2):
            for b in range(2):
                routes.append(((zl * 2 + a) * 2 + b, ((a * 4 + b * 2 + r) * 2 + c) * 2 + z))
    return routes


def local(queries, keys, values, out_weight, q_gain, k_gain, gate, valid_count):
    rows, width = queries.shape
    features = width * 16
    gathered = lax.all_gather(
        jnp.concatenate([keys, values], axis=1), "zl", axis=0, tiled=True, axis_index_groups=[RING]
    )
    weights = lax.ppermute(out_weight.T, ("zl", "core", "zh"), weight_routes())

    squares = jnp.stack(
        [
            jnp.sum(jnp.square(queries.astype(F32)), axis=1),
            jnp.sum(jnp.square(keys.astype(F32)), axis=1),
        ]
    )
    near = lax.all_to_all(
        jnp.broadcast_to(squares[None], (8, 2, rows)), ("y", "core"), 0, 0, tiled=True
    )
    near = jnp.sum(near, axis=0)
    totals = near + lax.ppermute(near, "zh", SWAP)
    inverse = lax.rsqrt(totals / features + EPSILON)
    key_inverse = lax.all_to_all(
        jnp.broadcast_to(inverse[1][None], (8, rows)), "zl", 0, 0, tiled=True
    )
    key_inverse = jnp.concatenate([key_inverse[z] for z in RING])[None, :]
    query_norm = (queries.astype(F32) * inverse[0][:, None] * q_gain[None, :]).astype(BF16)
    along_x = lax.all_gather(jnp.concatenate([query_norm, weights]), "x", axis=0, tiled=False)
    weights = lax.all_gather(
        along_x[:, rows:], "zl", axis=0, tiled=False, axis_index_groups=[RING]
    )

    limit = valid_count[0] - lax.axis_index("x") * (8 * rows)
    starts = np.repeat(np.asarray(RING, np.int32) * rows, rows)
    position = jnp.asarray(starts + np.tile(np.arange(rows, dtype=np.int32), 8))
    bias = jnp.where(position < limit, 0.0, BIAS).astype(F32)[None, :]
    parts = attention(along_x, gathered, key_inverse, bias, k_gain[:, None], rows)
    parts = lax.all_to_all(parts, "x", 0, 0, tiled=True)
    own = join(parts, width)
    across = lax.ppermute(own, "zh", SWAP)
    beside = lax.ppermute(own, "core", SWAP)
    both = lax.ppermute(across, "core", SWAP)
    place = jnp.stack([lax.axis_index("core"), lax.axis_index("zh")]).astype(jnp.int32)
    terms = project(place, (own, across, beside, both), weights)
    terms = lax.all_to_all(terms, "y", 0, 0, tiled=True)
    summed = jnp.sum(terms.astype(F32), axis=0)
    return (gate[None, :] * summed).astype(BF16)


def solution(mesh):
    fine = Mesh(mesh.devices.reshape(SIZES), AXES)
    tokens, features = ("x", "zl"), ("y", "core", "zh")
    placed = (
        P(tokens, features),
        P(tokens, features),
        P(tokens, features),
        P(features, tokens),
        P(features),
        P(features),
        P(features),
        P(),
    )
    return jax.shard_map(
        local, mesh=fine, in_specs=placed, out_specs=P(tokens, features), check_vma=False
    )
```

```python
import functools
import math

import jax
import jax.numpy as jnp
import numpy as np
from jax import lax
from jax.experimental import pallas as pl
from jax.experimental.pallas import tpu as pltpu
from jax.sharding import Mesh
from jax.sharding import PartitionSpec as P

HEAD_DIM = 128
EPSILON = 1e-06
BIAS = -1e30
F32 = jnp.float32
BF16 = jnp.bfloat16
AXES = ("x", "zl", "y", "core", "zh")
SIZES = (4, 8, 4, 2, 2)
SWAP = ((0, 1), (1, 0))
RING = [0, 2, 4, 6, 7, 5, 3, 1]


def attention_kernel(
    q_ref, kv_ref, inverse_ref, bias_ref, gain_ref, out_ref, kt_ref, ve_ref, *, heads, keys
):
    tile = q_ref.shape[1]
    factor = HEAD_DIM**-0.5 * math.log2(math.e)

    @pl.when(pl.program_id(0) == 0)
    def _():
        row = lax.broadcasted_iota(jnp.int32, (HEAD_DIM, keys), 0)
        bias = jnp.where(row == 0, bias_ref[...], 0.0).astype(BF16)
        for h in range(heads):
            columns = slice(h * HEAD_DIM, (h + 1) * HEAD_DIM)
            raw = kv_ref[:, columns].T.astype(F32)
            kt_ref[h, :HEAD_DIM, :] = (raw * inverse_ref[...] * gain_ref[columns, :]).astype(BF16)
            kt_ref[h, HEAD_DIM:, :] = bias
            ve_ref[h, :, :HEAD_DIM] = kv_ref[:, (heads + h) * HEAD_DIM : (heads + h + 1) * HEAD_DIM]
            ve_ref[h, :, HEAD_DIM:] = jnp.ones((keys, HEAD_DIM), BF16)

    lane = lax.broadcasted_iota(jnp.int32, (tile, HEAD_DIM), 1)
    first = jnp.where(lane == 0, 1.0, 0.0).astype(BF16)
    stats = jnp.zeros((tile, HEAD_DIM), F32)
    for h in range(heads):
        query = jnp.concatenate([q_ref[0, :, h * HEAD_DIM : (h + 1) * HEAD_DIM], first], axis=1)
        scores = jnp.dot(query, kt_ref[h], preferred_element_type=F32)
        top = (jnp.max(scores, axis=1, keepdims=True) * factor).astype(BF16).astype(F32)
        weights = jnp.exp2(scores * factor - top).astype(BF16)
        summed = jnp.dot(weights, ve_ref[h], preferred_element_type=F32)
        out_ref[0, :, h * HEAD_DIM : (h + 1) * HEAD_DIM] = summed[:, :HEAD_DIM].astype(BF16)
        mass = summed[:, HEAD_DIM:]
        high = mass.astype(BF16).astype(F32)
        stats = jnp.where(lane == 3 * h, top, stats)
        stats = jnp.where(lane == 3 * h + 1, high, stats)
        stats = jnp.where(lane == 3 * h + 2, mass - high, stats)
    out_ref[0, :, heads * HEAD_DIM :] = stats.astype(BF16)


def attention(queries, keys_values, inverse, bias, gain):
    blocks, rows, width = queries.shape
    keys = keys_values.shape[0]
    heads = width // HEAD_DIM
    return pl.pallas_call(
        functools.partial(attention_kernel, heads=heads, keys=keys),
        grid=(blocks,),
        in_specs=[
            pl.BlockSpec((1, rows, width), lambda i: (i, 0, 0)),
            pl.BlockSpec((keys, 2 * width), lambda i: (0, 0)),
            pl.BlockSpec((1, keys), lambda i: (0, 0)),
            pl.BlockSpec((1, keys), lambda i: (0, 0)),
            pl.BlockSpec((width, 1), lambda i: (0, 0)),
        ],
        out_specs=pl.BlockSpec((1, rows, width + HEAD_DIM), lambda i: (i, 0, 0)),
        out_shape=jax.ShapeDtypeStruct((blocks, rows, width + HEAD_DIM), BF16),
        scratch_shapes=[
            pltpu.VMEM((heads, 2 * HEAD_DIM, keys), BF16),
            pltpu.VMEM((heads, keys, 2 * HEAD_DIM), BF16),
        ],
        compiler_params=pltpu.CompilerParams(vmem_limit_bytes=48 << 20),
        cost_estimate=pl.CostEstimate(
            flops=8 * blocks * rows * keys * width,
            bytes_accessed=4 << 20,
            transcendentals=blocks * rows * keys * heads,
        ),
    )(queries, keys_values, inverse, bias, gain)


def join_kernel(parts_ref, out_ref, *, heads):
    count = parts_ref.shape[0]
    base = heads * HEAD_DIM
    for h in range(heads):
        tops = [parts_ref[i, :, base + 3 * h : base + 3 * h + 1].astype(F32) for i in range(count)]
        highest = functools.reduce(jnp.maximum, tops)
        total = jnp.zeros(out_ref.shape[:1] + (HEAD_DIM,), F32)
        mass = jnp.zeros_like(highest)
        for i in range(count):
            share = jnp.exp2(tops[i] - highest)
            part = parts_ref[i, :, base + 3 * h + 1 : base + 3 * h + 2].astype(F32)
            part = part + parts_ref[i, :, base + 3 * h + 2 : base + 3 * h + 3].astype(F32)
            mass = mass + share * part
            total = total + share * parts_ref[i, :, h * HEAD_DIM : (h + 1) * HEAD_DIM].astype(F32)
        out_ref[:, h * HEAD_DIM : (h + 1) * HEAD_DIM] = (total * (1.0 / mass)).astype(BF16)


def join(parts, width):
    return pl.pallas_call(
        functools.partial(join_kernel, heads=width // HEAD_DIM),
        out_shape=jax.ShapeDtypeStruct((parts.shape[1], width), BF16),
        compiler_params=pltpu.CompilerParams(vmem_limit_bytes=32 << 20),
    )(parts)


def project_kernel(place_ref, own_ref, zh_ref, core_ref, both_ref, weight_ref, out_ref):
    rows = out_ref.shape[1]
    core, zh = place_ref[0], place_ref[1]
    for r in range(2):
        total = jnp.zeros((rows, weight_ref.shape[2]), F32)
        for ref, a, b in (
            (own_ref, core, zh),
            (zh_ref, core, 1 - zh),
            (core_ref, 1 - core, zh),
            (both_ref, 1 - core, 1 - zh),
        ):
            pair = a * 2 + b
            block = weight_ref[0, pair if r == 0 else 7 - pair]
            total = total + lax.dot_general(
                ref[...], block, (((1,), (1,)), ((), ())), preferred_element_type=F32
            )
        out_ref[0, :, r * weight_ref.shape[2] : (r + 1) * weight_ref.shape[2]] = total.astype(BF16)


def project(place, pieces, weights):
    rows, width = pieces[0].shape
    groups, blocks, columns, _ = weights.shape
    whole = pl.BlockSpec((rows, width), lambda i: (0, 0))
    return pl.pallas_call(
        project_kernel,
        grid=(groups,),
        in_specs=[pl.BlockSpec(memory_space=pltpu.SMEM)]
        + [whole] * 4
        + [pl.BlockSpec((1, blocks, columns, width), lambda i: (i, 0, 0, 0))],
        out_specs=pl.BlockSpec((1, rows, 2 * columns), lambda i: (i, 0, 0)),
        out_shape=jax.ShapeDtypeStruct((groups, rows, 2 * columns), BF16),
        compiler_params=pltpu.CompilerParams(vmem_limit_bytes=32 << 20),
    )(place, *pieces, weights)


def weight_routes():
    routes = []
    for zl in range(8):
        c, z, r = zl // 4, zl // 2 % 2, zl % 2
        for a in range(2):
            for b in range(2):
                routes.append(((zl * 2 + a) * 2 + b, ((a * 4 + b * 2 + r) * 2 + c) * 2 + z))
    return routes


def pack(factors, width):
    high = lax.reduce_precision(factors, 8, 7)
    middle = lax.reduce_precision(factors - high, 8, 7)
    low = factors - high - middle
    lines = -(-factors.shape[0] // width)
    terms = jnp.stack([high, middle, low]).astype(BF16)
    terms = jnp.pad(terms, ((0, 0), (0, lines * width - factors.shape[0])))
    return jnp.pad(terms.reshape(3 * lines, width), ((0, 16 - 3 * lines), (0, 0)))


def unpack(packed, count):
    blocks, _, width = packed.shape
    lines = -(-count // width)
    terms = packed[:, : 3 * lines].astype(F32).reshape(blocks, 3, lines * width)
    return (terms[:, 0] + terms[:, 1] + terms[:, 2])[:, :count]


def local(queries, keys, values, out_weight, q_gain, k_gain, gate, valid_count):
    rows, width = queries.shape
    features = width * 16
    gathered = lax.all_gather(
        jnp.concatenate([keys, values], axis=1), "zl", axis=0, tiled=True, axis_index_groups=[RING]
    )
    weights = lax.ppermute(out_weight.T, ("zl", "core", "zh"), weight_routes())

    squares = jnp.stack(
        [
            jnp.sum(jnp.square(queries.astype(F32)), axis=1),
            jnp.sum(jnp.square(keys.astype(F32)), axis=1),
        ]
    )
    near = lax.all_to_all(
        jnp.broadcast_to(squares[None], (8, 2, rows)), ("y", "core"), 0, 0, tiled=True
    )
    near = jnp.sum(near, axis=0)
    totals = near + lax.ppermute(near, "zh", SWAP)
    inverse = lax.rsqrt(totals / features + EPSILON)
    query_norm = (queries.astype(F32) * inverse[0][:, None] * q_gain[None, :]).astype(BF16)
    query_all = lax.all_gather(query_norm, "x", axis=0, tiled=False)
    packed = jnp.concatenate([weights, pack(inverse[1], width)])
    along_zl = lax.all_gather(packed, "zl", axis=0, tiled=False, axis_index_groups=[RING])
    columns = weights.shape[0]
    key_inverse = unpack(along_zl[:, columns:], rows).reshape(1, 8 * rows)
    weights = lax.all_gather(along_zl[:, :columns], "x", axis=0, tiled=False)

    limit = valid_count[0] - lax.axis_index("x") * (8 * rows)
    starts = np.repeat(np.asarray(RING, np.int32) * rows, rows)
    position = jnp.asarray(starts + np.tile(np.arange(rows, dtype=np.int32), 8))
    bias = jnp.where(position < limit, 0.0, BIAS).astype(F32)[None, :]
    parts = attention(query_all, gathered, key_inverse, bias, k_gain[:, None])
    parts = lax.all_to_all(parts, "x", 0, 0, tiled=True)
    own = join(parts, width)
    across = lax.ppermute(own, "zh", SWAP)
    beside = lax.ppermute(own, "core", SWAP)
    both = lax.ppermute(across, "core", SWAP)
    place = jnp.stack([lax.axis_index("core"), lax.axis_index("zh")]).astype(jnp.int32)
    terms = project(place, (own, across, beside, both), weights)
    terms = lax.all_to_all(terms, "y", 0, 0, tiled=True)
    summed = jnp.sum(terms.astype(F32), axis=0)
    return (gate[None, :] * summed).astype(BF16)


def solution(mesh):
    fine = Mesh(mesh.devices.reshape(SIZES), AXES)
    tokens, features = ("x", "zl"), ("y", "core", "zh")
    placed = (
        P(tokens, features),
        P(tokens, features),
        P(tokens, features),
        P(features, tokens),
        P(features),
        P(features),
        P(features),
        P(),
    )
    return jax.shard_map(
        local, mesh=fine, in_specs=placed, out_specs=P(tokens, features), check_vma=False
    )
```

```python
import functools
import math

import jax
import jax.numpy as jnp
import numpy as np
from jax import lax
from jax.experimental import pallas as pl
from jax.experimental.pallas import tpu as pltpu
from jax.sharding import Mesh
from jax.sharding import PartitionSpec as P

HEAD_DIM = 128
EPSILON = 1e-06
BIAS = -1e30
F32 = jnp.float32
BF16 = jnp.bfloat16
AXES = ("xh", "xl", "zl", "y", "core", "zh")
SIZES = (2, 2, 8, 4, 2, 2)
X = ("xh", "xl")
SWAP = ((0, 1), (1, 0))
RING = [0, 2, 4, 6, 7, 5, 3, 1]


def attention_kernel(
    q_ref, kv_ref, inverse_ref, bias_ref, gain_ref, out_ref, kt_ref, ve_ref, *, rows, keys
):
    factor = HEAD_DIM**-0.5 * math.log2(math.e)
    odd = pl.program_id(0) % 2

    @pl.when(pl.program_id(0) == 0)
    def _():
        row = lax.broadcasted_iota(jnp.int32, (HEAD_DIM, keys), 0)
        bias = jnp.where(row == 0, bias_ref[...], 0.0).astype(BF16)
        for h in range(2):
            columns = slice(h * HEAD_DIM, (h + 1) * HEAD_DIM)
            raw = kv_ref[:, columns].T.astype(F32)
            kt_ref[h, :HEAD_DIM, :] = (raw * inverse_ref[...] * gain_ref[columns, :]).astype(BF16)
            kt_ref[h, HEAD_DIM:, :] = bias
            ve_ref[h, :, :HEAD_DIM] = kv_ref[:, (2 + h) * HEAD_DIM : (3 + h) * HEAD_DIM]
            ve_ref[h, :, HEAD_DIM:] = jnp.ones((keys, HEAD_DIM), BF16)

    lane = lax.broadcasted_iota(jnp.int32, (rows, HEAD_DIM), 1)
    first = jnp.where(lane == 0, 1.0, 0.0).astype(BF16)
    base = 3 * odd
    start = pl.multiple_of(odd * rows, 16)
    for h in range(2):
        query = jnp.concatenate([q_ref[0, h * rows : (h + 1) * rows, :], first], axis=1)
        scores = jnp.dot(query, kt_ref[h], preferred_element_type=F32)
        top = (jnp.max(scores, axis=1, keepdims=True) * factor).astype(BF16).astype(F32)
        weights = jnp.exp2(scores * factor - top).astype(BF16)
        summed = jnp.dot(weights, ve_ref[h], preferred_element_type=F32)
        out_ref[h, pl.ds(start, rows), :] = summed[:, :HEAD_DIM].astype(BF16)
        mass = summed[:, HEAD_DIM:]
        high = mass.astype(BF16).astype(F32)
        stats = jnp.where(lane == base, top, mass - high)
        stats = jnp.where(lane == base + 1, high, stats)
        kept = jnp.where(lane < base, out_ref[h, 2 * rows :, :].astype(F32), stats)
        out_ref[h, 2 * rows :, :] = kept.astype(BF16)


def attention(queries, keys_values, inverse, bias, gain, rows):
    blocks = queries.shape[0]
    keys = keys_values.shape[0]
    return pl.pallas_call(
        functools.partial(attention_kernel, rows=rows, keys=keys),
        grid=(blocks,),
        in_specs=[
            pl.BlockSpec((1, 2 * rows, HEAD_DIM), lambda i: (i, 0, 0)),
            pl.BlockSpec((keys, 4 * HEAD_DIM), lambda i: (0, 0)),
            pl.BlockSpec((1, keys), lambda i: (0, 0)),
            pl.BlockSpec((1, keys), lambda i: (0, 0)),
            pl.BlockSpec((2 * HEAD_DIM, 1), lambda i: (0, 0)),
        ],
        out_specs=pl.BlockSpec((2, 3 * rows, HEAD_DIM), lambda i: (i // 2, 0, 0)),
        out_shape=jax.ShapeDtypeStruct((blocks, 3 * rows, HEAD_DIM), BF16),
        scratch_shapes=[
            pltpu.VMEM((2, 2 * HEAD_DIM, keys), BF16),
            pltpu.VMEM((2, keys, 2 * HEAD_DIM), BF16),
        ],
        compiler_params=pltpu.CompilerParams(vmem_limit_bytes=48 << 20),
        cost_estimate=pl.CostEstimate(
            flops=16 * blocks * rows * keys * HEAD_DIM,
            bytes_accessed=4 << 20,
            transcendentals=2 * blocks * rows * keys,
        ),
    )(queries, keys_values, inverse, bias, gain)


def join_kernel(parts_ref, out_ref, *, rows):
    count = parts_ref.shape[0]
    for j in range(2):
        columns = [
            [parts_ref[i, 2 * rows :, 3 * j + n : 3 * j + n + 1].astype(F32) for n in range(3)]
            for i in range(count)
        ]
        highest = functools.reduce(jnp.maximum, [c[0] for c in columns])
        total = jnp.zeros((rows, HEAD_DIM), F32)
        mass = jnp.zeros_like(highest)
        for i in range(count):
            share = jnp.exp2(columns[i][0] - highest)
            mass = mass + share * (columns[i][1] + columns[i][2])
            total = total + share * parts_ref[i, j * rows : (j + 1) * rows, :].astype(F32)
        out_ref[j * rows : (j + 1) * rows, :] = (total * (1.0 / mass)).astype(BF16)


def join(parts, rows):
    return pl.pallas_call(
        functools.partial(join_kernel, rows=rows),
        out_shape=jax.ShapeDtypeStruct((2 * rows, HEAD_DIM), BF16),
        compiler_params=pltpu.CompilerParams(vmem_limit_bytes=32 << 20),
    )(parts)


def project_kernel(place_ref, own_ref, zh_ref, core_ref, both_ref, weight_ref, out_ref):
    rows, columns = out_ref.shape[2], weight_ref.shape[2]
    core, zh = place_ref[0], place_ref[1]
    for r in range(2):
        total = jnp.zeros((2 * rows, columns), F32)
        for ref, a, b in (
            (own_ref, core, zh),
            (zh_ref, core, 1 - zh),
            (core_ref, 1 - core, zh),
            (both_ref, 1 - core, 1 - zh),
        ):
            pair = a * 2 + b
            block = weight_ref[pair if r == 0 else 7 - pair, 0]
            total = total + lax.dot_general(
                ref[...], block, (((1,), (1,)), ((), ())), preferred_element_type=F32
            )
        for j in range(2):
            out_ref[j, 0, :, r * columns : (r + 1) * columns] = total[
                j * rows : (j + 1) * rows
            ].astype(BF16)


def project(place, pieces, weights):
    rows = pieces[0].shape[0] // 2
    blocks, groups, columns, depth = weights.shape
    whole = pl.BlockSpec((2 * rows, depth), lambda i: (0, 0))
    return pl.pallas_call(
        project_kernel,
        grid=(groups,),
        in_specs=[pl.BlockSpec(memory_space=pltpu.SMEM)]
        + [whole] * 4
        + [pl.BlockSpec((blocks, 1, columns, depth), lambda i: (0, i, 0, 0))],
        out_specs=pl.BlockSpec((2, 1, rows, 2 * columns), lambda i: (0, i, 0, 0)),
        out_shape=jax.ShapeDtypeStruct((2, groups, rows, 2 * columns), BF16),
        compiler_params=pltpu.CompilerParams(vmem_limit_bytes=32 << 20),
    )(place, *pieces, weights)


def weight_routes():
    routes = []
    for zl in range(8):
        c, z, r = zl // 4, zl // 2 % 2, zl % 2
        for a in range(2):
            for b in range(2):
                routes.append(((zl * 2 + a) * 2 + b, ((a * 4 + b * 2 + r) * 2 + c) * 2 + z))
    return routes


def local(queries, keys, values, out_weight, q_gain, k_gain, gate, valid_count):
    rows, width = queries.shape
    features = width * 16
    gathered = lax.all_gather(
        jnp.concatenate([keys, values], axis=1), "zl", axis=0, tiled=True, axis_index_groups=[RING]
    )
    weights = lax.ppermute(out_weight.T, ("zl", "core", "zh"), weight_routes())

    squares = jnp.stack(
        [
            jnp.sum(jnp.square(queries.astype(F32)), axis=1),
            jnp.sum(jnp.square(keys.astype(F32)), axis=1),
        ]
    )
    near = lax.all_to_all(
        jnp.broadcast_to(squares[None], (8, 2, rows)), ("y", "core"), 0, 0, tiled=True
    )
    near = jnp.sum(near, axis=0)
    totals = near + lax.ppermute(near, "zh", SWAP)
    inverse = lax.rsqrt(totals / features + EPSILON)
    key_inverse = lax.all_to_all(
        jnp.broadcast_to(inverse[1][None], (8, rows)), "zl", 0, 0, tiled=True
    )
    key_inverse = jnp.concatenate([key_inverse[z] for z in RING])[None, :]
    query_norm = (queries.astype(F32) * inverse[0][:, None] * q_gain[None, :]).astype(BF16)
    heads = [query_norm[:, :HEAD_DIM], query_norm[:, HEAD_DIM:]]
    to_even = jnp.concatenate(heads + [weights[:, :HEAD_DIM]])
    to_odd = jnp.concatenate(heads + [weights[:, HEAD_DIM:]])
    along_x = lax.all_to_all(
        jnp.stack([to_even, to_odd, to_even, to_odd]), X, 0, 0, tiled=True
    )
    weights = lax.all_gather(
        along_x[:, 2 * rows :], "zl", axis=0, tiled=False, axis_index_groups=[RING]
    )

    place_x = lax.axis_index("xh") * 2 + lax.axis_index("xl")
    limit = valid_count[0] - place_x * (8 * rows)
    starts = np.repeat(np.asarray(RING, np.int32) * rows, rows)
    position = jnp.asarray(starts + np.tile(np.arange(rows, dtype=np.int32), 8))
    bias = jnp.where(position < limit, 0.0, BIAS).astype(F32)[None, :]
    parts = attention(along_x, gathered, key_inverse, bias, k_gain[:, None], rows)
    parts = lax.all_to_all(parts, X, 0, 0, tiled=True)
    own = join(parts, rows)
    across = lax.ppermute(own, "zh", SWAP)
    beside = lax.ppermute(own, "core", SWAP)
    both = lax.ppermute(across, "core", SWAP)
    place = jnp.stack([lax.axis_index("core"), lax.axis_index("zh")]).astype(jnp.int32)
    terms = project(place, (own, across, beside, both), weights)
    terms = lax.all_to_all(terms.reshape(8, rows, -1), ("xl", "y"), 0, 0, tiled=True)
    summed = jnp.sum(terms.astype(F32), axis=0)
    return (gate[None, :] * summed).astype(BF16)


def solution(mesh):
    fine = Mesh(mesh.devices.reshape(SIZES), AXES)
    tokens, features = ("xh", "xl", "zl"), ("y", "core", "zh")
    placed = (
        P(tokens, features),
        P(tokens, features),
        P(tokens, features),
        P(features, tokens),
        P(features),
        P(features),
        P(features),
        P(),
    )
    return jax.shard_map(
        local, mesh=fine, in_specs=placed, out_specs=P(tokens, features), check_vma=False
    )
```

```python
import functools
import math

import jax
import jax.numpy as jnp
import numpy as np
from jax import lax
from jax.experimental import pallas as pl
from jax.experimental.pallas import tpu as pltpu
from jax.sharding import Mesh
from jax.sharding import PartitionSpec as P

HEAD_DIM = 128
EPSILON = 1e-06
BIAS = -1e30
F32 = jnp.float32
BF16 = jnp.bfloat16
AXES = ("x", "zl", "y", "core", "zh")
SIZES = (4, 8, 4, 2, 2)
SWAP = ((0, 1), (1, 0))
RING = [0, 2, 4, 6, 7, 5, 3, 1]
LARGE = 112


def attention_kernel(
    q_ref, kv_ref, inverse_ref, bias_ref, gain_ref, out_ref, kt_ref, ve_ref, *, heads, keys
):
    tile = q_ref.shape[1]
    factor = HEAD_DIM**-0.5 * math.log2(math.e)

    @pl.when(pl.program_id(0) == 0)
    def _():
        row = lax.broadcasted_iota(jnp.int32, (HEAD_DIM, keys), 0)
        bias = jnp.where(row == 0, bias_ref[...], 0.0).astype(BF16)
        for h in range(heads):
            columns = slice(h * HEAD_DIM, (h + 1) * HEAD_DIM)
            raw = kv_ref[:, columns].T.astype(F32)
            kt_ref[h, :HEAD_DIM, :] = (raw * inverse_ref[...] * gain_ref[columns, :]).astype(BF16)
            kt_ref[h, HEAD_DIM:, :] = bias
            ve_ref[h, :, :HEAD_DIM] = kv_ref[:, (heads + h) * HEAD_DIM : (heads + h + 1) * HEAD_DIM]
            ve_ref[h, :, HEAD_DIM:] = jnp.ones((keys, HEAD_DIM), BF16)

    lane = lax.broadcasted_iota(jnp.int32, (tile, HEAD_DIM), 1)
    first = jnp.where(lane == 0, 1.0, 0.0).astype(BF16)
    stats = jnp.zeros((tile, HEAD_DIM), F32)
    for h in range(heads):
        query = jnp.concatenate([q_ref[0, :, h * HEAD_DIM : (h + 1) * HEAD_DIM], first], axis=1)
        scores = jnp.dot(query, kt_ref[h], preferred_element_type=F32)
        top = (jnp.max(scores, axis=1, keepdims=True) * factor).astype(BF16).astype(F32)
        weights = jnp.exp2(scores * factor - top).astype(BF16)
        summed = jnp.dot(weights, ve_ref[h], preferred_element_type=F32)
        out_ref[0, :, h * HEAD_DIM : (h + 1) * HEAD_DIM] = summed[:, :HEAD_DIM].astype(BF16)
        mass = summed[:, HEAD_DIM:]
        high = mass.astype(BF16).astype(F32)
        stats = jnp.where(lane == 3 * h, top, stats)
        stats = jnp.where(lane == 3 * h + 1, high, stats)
        stats = jnp.where(lane == 3 * h + 2, mass - high, stats)
    out_ref[0, :, heads * HEAD_DIM :] = stats.astype(BF16)


def attention(queries, keys_values, inverse, bias, gain):
    blocks, rows, width = queries.shape
    keys = keys_values.shape[0]
    heads = width // HEAD_DIM
    return pl.pallas_call(
        functools.partial(attention_kernel, heads=heads, keys=keys),
        grid=(blocks,),
        in_specs=[
            pl.BlockSpec((1, rows, width), lambda i: (i, 0, 0)),
            pl.BlockSpec((keys, 2 * width), lambda i: (0, 0)),
            pl.BlockSpec((1, keys), lambda i: (0, 0)),
            pl.BlockSpec((1, keys), lambda i: (0, 0)),
            pl.BlockSpec((width, 1), lambda i: (0, 0)),
        ],
        out_specs=pl.BlockSpec((1, rows, width + HEAD_DIM), lambda i: (i, 0, 0)),
        out_shape=jax.ShapeDtypeStruct((blocks, rows, width + HEAD_DIM), BF16),
        scratch_shapes=[
            pltpu.VMEM((heads, 2 * HEAD_DIM, keys), BF16),
            pltpu.VMEM((heads, keys, 2 * HEAD_DIM), BF16),
        ],
        compiler_params=pltpu.CompilerParams(vmem_limit_bytes=48 << 20),
        cost_estimate=pl.CostEstimate(
            flops=8 * blocks * rows * keys * width,
            bytes_accessed=4 << 20,
            transcendentals=blocks * rows * keys * heads,
        ),
    )(queries, keys_values, inverse, bias, gain)


def join_kernel(parts_ref, out_ref, *, heads):
    count = parts_ref.shape[0]
    base = heads * HEAD_DIM
    for h in range(heads):
        tops = [parts_ref[i, :, base + 3 * h : base + 3 * h + 1].astype(F32) for i in range(count)]
        highest = functools.reduce(jnp.maximum, tops)
        total = jnp.zeros(out_ref.shape[:1] + (HEAD_DIM,), F32)
        mass = jnp.zeros_like(highest)
        for i in range(count):
            share = jnp.exp2(tops[i] - highest)
            part = parts_ref[i, :, base + 3 * h + 1 : base + 3 * h + 2].astype(F32)
            part = part + parts_ref[i, :, base + 3 * h + 2 : base + 3 * h + 3].astype(F32)
            mass = mass + share * part
            total = total + share * parts_ref[i, :, h * HEAD_DIM : (h + 1) * HEAD_DIM].astype(F32)
        out_ref[:, h * HEAD_DIM : (h + 1) * HEAD_DIM] = (total * (1.0 / mass)).astype(BF16)


def join(parts, width):
    return pl.pallas_call(
        functools.partial(join_kernel, heads=width // HEAD_DIM),
        out_shape=jax.ShapeDtypeStruct((parts.shape[1], width), BF16),
        compiler_params=pltpu.CompilerParams(vmem_limit_bytes=32 << 20),
    )(parts)


def project_kernel(
    place_ref, own_ref, zh_ref, core_ref, both_ref, large_ref, small_ref, out_ref
):
    rows = out_ref.shape[1]
    columns = out_ref.shape[2] // 2
    core, zh = place_ref[0], place_ref[1]
    for r in range(2):
        total = jnp.zeros((rows, columns), F32)
        for ref, a, b in (
            (own_ref, core, zh),
            (zh_ref, core, 1 - zh),
            (core_ref, 1 - core, zh),
            (both_ref, 1 - core, 1 - zh),
        ):
            pair = a * 2 + b
            spot = pair if r == 0 else 7 - pair
            block = jnp.concatenate([large_ref[0, spot], small_ref[0, spot]])
            total = total + lax.dot_general(
                ref[...], block, (((1,), (1,)), ((), ())), preferred_element_type=F32
            )
        out_ref[0, :, r * columns : (r + 1) * columns] = total.astype(BF16)


def project(place, pieces, large, small):
    rows, width = pieces[0].shape
    groups, blocks = large.shape[:2]
    columns = large.shape[2] + small.shape[2]
    whole = pl.BlockSpec((rows, width), lambda i: (0, 0))
    return pl.pallas_call(
        project_kernel,
        grid=(groups,),
        in_specs=[pl.BlockSpec(memory_space=pltpu.SMEM)]
        + [whole] * 4
        + [pl.BlockSpec((1,) + w.shape[1:], lambda i: (i, 0, 0, 0)) for w in (large, small)],
        out_specs=pl.BlockSpec((1, rows, 2 * columns), lambda i: (i, 0, 0)),
        out_shape=jax.ShapeDtypeStruct((groups, rows, 2 * columns), BF16),
        compiler_params=pltpu.CompilerParams(vmem_limit_bytes=32 << 20),
    )(place, *pieces, large, small)


def weight_routes():
    routes = []
    for zl in range(8):
        c, z, r = zl // 4, zl // 2 % 2, zl % 2
        for a in range(2):
            for b in range(2):
                routes.append(((zl * 2 + a) * 2 + b, ((a * 4 + b * 2 + r) * 2 + c) * 2 + z))
    return routes


def local(queries, keys, values, out_weight, q_gain, k_gain, gate, valid_count):
    rows, width = queries.shape
    features = width * 16
    gathered = lax.all_gather(
        jnp.concatenate([keys, values], axis=1), "zl", axis=0, tiled=True, axis_index_groups=[RING]
    )
    columns = out_weight.shape[1]
    weights = lax.ppermute(out_weight.T, ("zl", "core", "zh"), weight_routes())
    weights = lax.all_gather(
        jnp.pad(weights, ((0, 256 - columns), (0, 0))),
        "zl",
        axis=0,
        tiled=False,
        axis_index_groups=[RING],
    )

    squares = jnp.stack(
        [
            jnp.sum(jnp.square(queries.astype(F32)), axis=1),
            jnp.sum(jnp.square(keys.astype(F32)), axis=1),
        ]
    )
    near = lax.all_to_all(
        jnp.broadcast_to(squares[None], (8, 2, rows)), ("y", "core"), 0, 0, tiled=True
    )
    near = jnp.sum(near, axis=0)
    totals = near + lax.ppermute(near, "zh", SWAP)
    inverse = lax.rsqrt(totals / features + EPSILON)
    key_inverse = lax.all_to_all(
        jnp.broadcast_to(inverse[1][None], (8, rows)), "zl", 0, 0, tiled=True
    )
    key_inverse = jnp.concatenate([key_inverse[z] for z in RING])[None, :]
    query_norm = (queries.astype(F32) * inverse[0][:, None] * q_gain[None, :]).astype(BF16)
    query_all = lax.all_gather(query_norm, "x", axis=0, tiled=False)

    limit = valid_count[0] - lax.axis_index("x") * (8 * rows)
    starts = np.repeat(np.asarray(RING, np.int32) * rows, rows)
    position = jnp.asarray(starts + np.tile(np.arange(rows, dtype=np.int32), 8))
    bias = jnp.where(position < limit, 0.0, BIAS).astype(F32)[None, :]
    parts = attention(query_all, gathered, key_inverse, bias, k_gain[:, None])
    parts = lax.all_to_all(parts, "x", 0, 0, tiled=True)
    own = join(parts, width)
    own, weights = lax.optimization_barrier((own, weights))
    large = lax.all_gather(weights[:, :LARGE], "x", axis=0, tiled=False)
    small = lax.all_gather(weights[:, LARGE:columns], "x", axis=0, tiled=False)
    across = lax.ppermute(own, "zh", SWAP)
    beside = lax.ppermute(own, "core", SWAP)
    across, small = lax.optimization_barrier((across, small))
    both = lax.ppermute(across, "core", SWAP)
    place = jnp.stack([lax.axis_index("core"), lax.axis_index("zh")]).astype(jnp.int32)
    terms = project(place, (own, across, beside, both), large, small)
    terms = lax.all_to_all(terms, "y", 0, 0, tiled=True)
    summed = jnp.sum(terms.astype(F32), axis=0)
    return (gate[None, :] * summed).astype(BF16)


def solution(mesh):
    fine = Mesh(mesh.devices.reshape(SIZES), AXES)
    tokens, features = ("x", "zl"), ("y", "core", "zh")
    placed = (
        P(tokens, features),
        P(tokens, features),
        P(tokens, features),
        P(features, tokens),
        P(features),
        P(features),
        P(features),
        P(),
    )
    return jax.shard_map(
        local, mesh=fine, in_specs=placed, out_specs=P(tokens, features), check_vma=False
    )
```

```python
import functools
import math

import jax
import jax.numpy as jnp
import numpy as np
from jax import lax
from jax.experimental import pallas as pl
from jax.experimental.pallas import tpu as pltpu
from jax.sharding import Mesh
from jax.sharding import PartitionSpec as P

HEAD_DIM = 128
EPSILON = 1e-06
BIAS = -1e30
F32 = jnp.float32
BF16 = jnp.bfloat16
AXES = ("x", "zl", "y", "core", "zh")
SIZES = (4, 8, 4, 2, 2)
SWAP = ((0, 1), (1, 0))
RING = [0, 2, 4, 6, 7, 5, 3, 1]


def attention_kernel(
    q_ref, kv_ref, inverse_ref, bias_ref, gain_ref, out_ref, kt_ref, ve_ref, *, heads, keys
):
    tile = q_ref.shape[1]
    factor = HEAD_DIM**-0.5 * math.log2(math.e)

    @pl.when(pl.program_id(0) == 0)
    def _():
        row = lax.broadcasted_iota(jnp.int32, (HEAD_DIM, keys), 0)
        bias = jnp.where(row == 0, bias_ref[...], 0.0).astype(BF16)
        for h in range(heads):
            columns = slice(h * HEAD_DIM, (h + 1) * HEAD_DIM)
            raw = kv_ref[:, columns].T.astype(F32)
            kt_ref[h, :HEAD_DIM, :] = (raw * inverse_ref[...] * gain_ref[columns, :]).astype(BF16)
            kt_ref[h, HEAD_DIM:, :] = bias
            ve_ref[h, :, :HEAD_DIM] = kv_ref[:, (heads + h) * HEAD_DIM : (heads + h + 1) * HEAD_DIM]
            ve_ref[h, :, HEAD_DIM:] = jnp.ones((keys, HEAD_DIM), BF16)

    lane = lax.broadcasted_iota(jnp.int32, (tile, HEAD_DIM), 1)
    first = jnp.where(lane == 0, 1.0, 0.0).astype(BF16)
    stats = jnp.zeros((tile, HEAD_DIM), F32)
    for h in range(heads):
        query = jnp.concatenate([q_ref[0, :, h * HEAD_DIM : (h + 1) * HEAD_DIM], first], axis=1)
        scores = jnp.dot(query, kt_ref[h], preferred_element_type=F32)
        top = (jnp.max(scores, axis=1, keepdims=True) * factor).astype(BF16).astype(F32)
        weights = jnp.exp2(scores * factor - top).astype(BF16)
        summed = jnp.dot(weights, ve_ref[h], preferred_element_type=F32)
        out_ref[0, :, h * HEAD_DIM : (h + 1) * HEAD_DIM] = summed[:, :HEAD_DIM].astype(BF16)
        mass = summed[:, HEAD_DIM:]
        high = mass.astype(BF16).astype(F32)
        stats = jnp.where(lane == 3 * h, top, stats)
        stats = jnp.where(lane == 3 * h + 1, high, stats)
        stats = jnp.where(lane == 3 * h + 2, mass - high, stats)
    out_ref[0, :, heads * HEAD_DIM :] = stats.astype(BF16)


def attention(queries, keys_values, inverse, bias, gain, rows):
    blocks, _, width = queries.shape
    keys = keys_values.shape[0]
    heads = width // HEAD_DIM
    return pl.pallas_call(
        functools.partial(attention_kernel, heads=heads, keys=keys),
        grid=(blocks,),
        in_specs=[
            pl.BlockSpec((1, rows, width), lambda i: (i, 0, 0)),
            pl.BlockSpec((keys, 2 * width), lambda i: (0, 0)),
            pl.BlockSpec((1, keys), lambda i: (0, 0)),
            pl.BlockSpec((1, keys), lambda i: (0, 0)),
            pl.BlockSpec((width, 1), lambda i: (0, 0)),
        ],
        out_specs=pl.BlockSpec((1, rows, width + HEAD_DIM), lambda i: (i, 0, 0)),
        out_shape=jax.ShapeDtypeStruct((blocks, rows, width + HEAD_DIM), BF16),
        scratch_shapes=[
            pltpu.VMEM((heads, 2 * HEAD_DIM, keys), BF16),
            pltpu.VMEM((heads, keys, 2 * HEAD_DIM), BF16),
        ],
        compiler_params=pltpu.CompilerParams(vmem_limit_bytes=48 << 20),
        cost_estimate=pl.CostEstimate(
            flops=8 * blocks * rows * keys * width,
            bytes_accessed=4 << 20,
            transcendentals=blocks * rows * keys * heads,
        ),
    )(queries, keys_values, inverse, bias, gain)


def join_kernel(parts_ref, out_ref, *, heads):
    count = parts_ref.shape[0]
    base = heads * HEAD_DIM
    for h in range(heads):
        tops = [parts_ref[i, :, base + 3 * h : base + 3 * h + 1].astype(F32) for i in range(count)]
        highest = functools.reduce(jnp.maximum, tops)
        total = jnp.zeros(out_ref.shape[:1] + (HEAD_DIM,), F32)
        mass = jnp.zeros_like(highest)
        for i in range(count):
            share = jnp.exp2(tops[i] - highest)
            part = parts_ref[i, :, base + 3 * h + 1 : base + 3 * h + 2].astype(F32)
            part = part + parts_ref[i, :, base + 3 * h + 2 : base + 3 * h + 3].astype(F32)
            mass = mass + share * part
            total = total + share * parts_ref[i, :, h * HEAD_DIM : (h + 1) * HEAD_DIM].astype(F32)
        out_ref[:, h * HEAD_DIM : (h + 1) * HEAD_DIM] = (total * (1.0 / mass)).astype(BF16)


def join(parts, width):
    return pl.pallas_call(
        functools.partial(join_kernel, heads=width // HEAD_DIM),
        out_shape=jax.ShapeDtypeStruct((parts.shape[1], width), BF16),
        compiler_params=pltpu.CompilerParams(vmem_limit_bytes=32 << 20),
    )(parts)


def project_kernel(
    place_ref, own_ref, core_ref, zh_ref, both_ref, weight_ref, gate_ref, out_ref, total_ref
):
    columns = weight_ref.shape[2]
    core, zh = place_ref[0], place_ref[1]
    step = pl.program_id(0)
    for r in range(2):
        total = jnp.zeros((out_ref.shape[0], columns), F32)
        for ref, a, b in (
            (own_ref, core, zh),
            (core_ref, 1 - core, zh),
            (zh_ref, core, 1 - zh),
            (both_ref, 1 - core, 1 - zh),
        ):
            pair = a * 2 + b
            block = weight_ref[pair if r == 0 else 7 - pair, 0]
            total = total + lax.dot_general(
                ref[0], block, (((1,), (1,)), ((), ())), preferred_element_type=F32
            )

        @pl.when(step == 0)
        def _():
            total_ref[r] = total

        @pl.when(step > 0)
        def _():
            total_ref[r] += total

    @pl.when(step == pl.num_programs(0) - 1)
    def _():
        for r in range(2):
            span = slice(r * columns, (r + 1) * columns)
            out_ref[:, span] = (total_ref[r] * gate_ref[:, span]).astype(BF16)


def project(place, pieces, weights, gate):
    groups, rows, width = pieces[0].shape
    blocks, _, columns, _ = weights.shape
    return pl.pallas_call(
        project_kernel,
        grid=(groups,),
        in_specs=[pl.BlockSpec(memory_space=pltpu.SMEM)]
        + [pl.BlockSpec((1, rows, width), lambda i: (i, 0, 0))] * 4
        + [
            pl.BlockSpec((blocks, 1, columns, width), lambda i: (0, i, 0, 0)),
            pl.BlockSpec((1, 2 * columns), lambda i: (0, 0)),
        ],
        out_specs=pl.BlockSpec((rows, 2 * columns), lambda i: (0, 0)),
        out_shape=jax.ShapeDtypeStruct((rows, 2 * columns), BF16),
        scratch_shapes=[pltpu.VMEM((2, rows, columns), F32)],
        compiler_params=pltpu.CompilerParams(vmem_limit_bytes=32 << 20),
    )(place, *pieces, weights, gate)


def weight_routes():
    routes = []
    for x, zl, y, a, b in np.ndindex(*SIZES):
        c, z, r = zl // 4, zl // 2 % 2, zl % 2
        target = (y, a * 4 + b * 2 + r, x, c, z)
        routes.append(
            (int(np.ravel_multi_index((x, zl, y, a, b), SIZES)), int(np.ravel_multi_index(target, SIZES)))
        )
    return routes


def local(queries, keys, values, out_weight, q_gain, k_gain, gate, valid_count):
    rows, width = queries.shape
    features = width * 16
    gathered = lax.all_gather(
        jnp.concatenate([keys, values], axis=1), "zl", axis=0, tiled=True, axis_index_groups=[RING]
    )
    weights = lax.ppermute(out_weight.T, AXES, weight_routes())

    squares = jnp.stack(
        [
            jnp.sum(jnp.square(queries.astype(F32)), axis=1),
            jnp.sum(jnp.square(keys.astype(F32)), axis=1),
        ]
    )
    near = lax.all_to_all(
        jnp.broadcast_to(squares[None], (8, 2, rows)), ("y", "core"), 0, 0, tiled=True
    )
    near = jnp.sum(near, axis=0)
    totals = near + lax.ppermute(near, "zh", SWAP)
    inverse = lax.rsqrt(totals / features + EPSILON)
    key_inverse = lax.all_to_all(
        jnp.broadcast_to(inverse[1][None], (8, rows)), "zl", 0, 0, tiled=True
    )
    key_inverse = jnp.concatenate([key_inverse[z] for z in RING])[None, :]
    query_norm = (queries.astype(F32) * inverse[0][:, None] * q_gain[None, :]).astype(BF16)
    along_x = lax.all_gather(jnp.concatenate([query_norm, weights]), "x", axis=0, tiled=False)
    weights = lax.all_gather(
        along_x[:, rows:], "zl", axis=0, tiled=False, axis_index_groups=[RING]
    )

    limit = valid_count[0] - lax.axis_index("x") * (8 * rows)
    starts = np.repeat(np.asarray(RING, np.int32) * rows, rows)
    position = jnp.asarray(starts + np.tile(np.arange(rows, dtype=np.int32), 8))
    bias = jnp.where(position < limit, 0.0, BIAS).astype(F32)[None, :]
    parts = attention(along_x, gathered, key_inverse, bias, k_gain[:, None], rows)
    parts = lax.all_to_all(parts, "x", 0, 0, tiled=True)
    own = join(parts, width)
    across = lax.ppermute(own, "zh", SWAP)
    own_y = lax.all_gather(own, "y", axis=0, tiled=False)
    beside_y = lax.ppermute(own_y, "core", SWAP)
    across_y = lax.all_gather(across, "y", axis=0, tiled=False)
    both_y = lax.ppermute(across_y, "core", SWAP)
    place = jnp.stack([lax.axis_index("core"), lax.axis_index("zh")]).astype(jnp.int32)
    return project(place, (own_y, beside_y, across_y, both_y), weights, gate[None, :])


def solution(mesh):
    fine = Mesh(mesh.devices.reshape(SIZES), AXES)
    tokens, features = ("x", "zl"), ("y", "core", "zh")
    placed = (
        P(tokens, features),
        P(tokens, features),
        P(tokens, features),
        P(features, tokens),
        P(features),
        P(features),
        P(features),
        P(),
    )
    return jax.shard_map(
        local, mesh=fine, in_specs=placed, out_specs=P(tokens, features), check_vma=False
    )
```

```python
import functools
import math

import jax
import jax.numpy as jnp
import numpy as np
from jax import lax
from jax.experimental import pallas as pl
from jax.experimental.pallas import tpu as pltpu
from jax.sharding import Mesh
from jax.sharding import PartitionSpec as P

HEAD_DIM = 128
EPSILON = 1e-06
BIAS = -1e30
F32 = jnp.float32
BF16 = jnp.bfloat16
AXES = ("x", "zl", "y", "core", "zh")
SIZES = (4, 8, 4, 2, 2)
SWAP = ((0, 1), (1, 0))
RING = [0, 2, 4, 6, 7, 5, 3, 1]


def attention_kernel(
    q_ref, kv_ref, inverse_ref, bias_ref, gain_ref, out_ref, kt_ref, ve_ref
):
    factor = HEAD_DIM**-0.5 * math.log2(math.e)
    blocks, rows, width = q_ref.shape
    keys = kv_ref.shape[0]
    row = lax.broadcasted_iota(jnp.int32, (HEAD_DIM, keys), 0)
    bias = jnp.where(row == 0, bias_ref[...], 0.0).astype(BF16)
    for h in range(2):
        columns = slice(h * HEAD_DIM, (h + 1) * HEAD_DIM)
        raw = kv_ref[:, columns].T.astype(F32)
        kt_ref[h, :HEAD_DIM, :] = (raw * inverse_ref[...] * gain_ref[columns, :]).astype(BF16)
        kt_ref[h, HEAD_DIM:, :] = bias
        ve_ref[h, :, :HEAD_DIM] = kv_ref[:, (2 + h) * HEAD_DIM : (3 + h) * HEAD_DIM]
        ve_ref[h, :, HEAD_DIM:] = jnp.ones((keys, HEAD_DIM), BF16)

    lane = lax.broadcasted_iota(jnp.int32, (rows, HEAD_DIM), 1)
    first = jnp.where(lane == 0, 1.0, 0.0).astype(BF16)
    for b in range(blocks):
        stats = jnp.zeros((rows, HEAD_DIM), F32)
        scores = []
        for h in range(2):
            query = jnp.concatenate([q_ref[b, :, h * HEAD_DIM : (h + 1) * HEAD_DIM], first], axis=1)
            scores.append(jnp.dot(query, kt_ref[h], preferred_element_type=F32))
        for h in range(2):
            top = (jnp.max(scores[h], axis=1, keepdims=True) * factor).astype(BF16).astype(F32)
            weights = jnp.exp2(scores[h] * factor - top).astype(BF16)
            summed = jnp.dot(weights, ve_ref[h], preferred_element_type=F32)
            out_ref[b, :rows, h * HEAD_DIM : (h + 1) * HEAD_DIM] = summed[:, :HEAD_DIM].astype(BF16)
            mass = summed[:, HEAD_DIM:]
            high = mass.astype(BF16).astype(F32)
            stats = jnp.where(lane == 3 * h, top, stats)
            stats = jnp.where(lane == 3 * h + 1, high, stats)
            stats = jnp.where(lane == 3 * h + 2, mass - high, stats)
        lines = stats.T[:8]
        rest = jnp.pad(lines[:, width:], ((0, 0), (0, 2 * width - rows)))
        out_ref[b, rows:, :] = jnp.concatenate([lines[:, :width], rest]).astype(BF16)


def attention(queries, keys_values, inverse, bias, gain):
    blocks, rows, width = queries.shape
    keys = keys_values.shape[0]
    return pl.pallas_call(
        attention_kernel,
        grid=(1,),
        in_specs=[
            pl.BlockSpec((blocks, rows, width), lambda i: (0, 0, 0)),
            pl.BlockSpec((keys, 2 * width), lambda i: (0, 0)),
            pl.BlockSpec((1, keys), lambda i: (0, 0)),
            pl.BlockSpec((1, keys), lambda i: (0, 0)),
            pl.BlockSpec((width, 1), lambda i: (0, 0)),
        ],
        out_specs=pl.BlockSpec((blocks, rows + 16, width), lambda i: (0, 0, 0)),
        out_shape=jax.ShapeDtypeStruct((blocks, rows + 16, width), BF16),
        scratch_shapes=[
            pltpu.VMEM((2, 2 * HEAD_DIM, keys), BF16),
            pltpu.VMEM((2, keys, 2 * HEAD_DIM), BF16),
        ],
        compiler_params=pltpu.CompilerParams(vmem_limit_bytes=48 << 20),
        cost_estimate=pl.CostEstimate(
            flops=8 * blocks * rows * keys * width,
            bytes_accessed=4 << 20,
            transcendentals=2 * blocks * rows * keys,
        ),
    )(queries, keys_values, inverse, bias, gain)


def join_kernel(parts_ref, out_ref):
    count = parts_ref.shape[0]
    rows = out_ref.shape[0]
    lines = []
    for i in range(count):
        packed = parts_ref[i, rows:, :].astype(F32)
        lines.append(jnp.concatenate([packed[:8, :], packed[8:, :128]], axis=1))
    shares = []
    for h in range(2):
        tops = [line[3 * h : 3 * h + 1] for line in lines]
        highest = functools.reduce(jnp.maximum, tops)
        weights = [jnp.exp2(top - highest) for top in tops]
        mass = sum(
            w * (line[3 * h + 1 : 3 * h + 2] + line[3 * h + 2 : 3 * h + 3])
            for w, line in zip(weights, lines)
        )
        mass = jnp.where(mass == 0.0, 1.0, mass)
        shares += [w / mass for w in weights]
    spread = jnp.zeros((HEAD_DIM - 2 * count, lines[0].shape[1]), F32)
    columns = jnp.concatenate(shares + [spread]).T
    for h in range(2):
        span = slice(h * HEAD_DIM, (h + 1) * HEAD_DIM)
        total = jnp.zeros((rows, HEAD_DIM), F32)
        for i in range(count):
            share = columns[:rows, h * count + i : h * count + i + 1]
            total = total + share * parts_ref[i, :rows, span].astype(F32)
        out_ref[:, span] = total.astype(BF16)


def join(parts):
    return pl.pallas_call(
        join_kernel,
        out_shape=jax.ShapeDtypeStruct((parts.shape[1] - 16, parts.shape[2]), BF16),
        compiler_params=pltpu.CompilerParams(vmem_limit_bytes=32 << 20),
    )(parts)


def project_kernel(
    place_ref, own_ref, core_ref, zh_ref, both_ref, weight_ref, gate_ref, out_ref, total_ref
):
    columns = weight_ref.shape[2]
    core, zh = place_ref[0], place_ref[1]
    step = pl.program_id(0)
    for r in range(2):
        total = jnp.zeros((out_ref.shape[0], columns), F32)
        for ref, a, b in (
            (own_ref, core, zh),
            (core_ref, 1 - core, zh),
            (zh_ref, core, 1 - zh),
            (both_ref, 1 - core, 1 - zh),
        ):
            pair = a * 2 + b
            block = weight_ref[pair if r == 0 else 7 - pair, 0]
            total = total + lax.dot_general(
                ref[0], block, (((1,), (1,)), ((), ())), preferred_element_type=F32
            )

        @pl.when(step == 0)
        def _():
            total_ref[r] = total

        @pl.when(step > 0)
        def _():
            total_ref[r] += total

    @pl.when(step == pl.num_programs(0) - 1)
    def _():
        for r in range(2):
            span = slice(r * columns, (r + 1) * columns)
            out_ref[:, span] = (total_ref[r] * gate_ref[:, span]).astype(BF16)


def project(place, pieces, weights, gate):
    groups, rows, width = pieces[0].shape
    blocks, _, columns, _ = weights.shape
    return pl.pallas_call(
        project_kernel,
        grid=(groups,),
        in_specs=[pl.BlockSpec(memory_space=pltpu.SMEM)]
        + [pl.BlockSpec((1, rows, width), lambda i: (i, 0, 0))] * 4
        + [
            pl.BlockSpec((blocks, 1, columns, width), lambda i: (0, i, 0, 0)),
            pl.BlockSpec((1, 2 * columns), lambda i: (0, 0)),
        ],
        out_specs=pl.BlockSpec((rows, 2 * columns), lambda i: (0, 0)),
        out_shape=jax.ShapeDtypeStruct((rows, 2 * columns), BF16),
        scratch_shapes=[pltpu.VMEM((2, rows, columns), F32)],
        compiler_params=pltpu.CompilerParams(vmem_limit_bytes=32 << 20),
    )(place, *pieces, weights, gate)


def weight_routes():
    routes = []
    for x, zl, y, a, b in np.ndindex(*SIZES):
        c, z, r = zl // 4, zl // 2 % 2, zl % 2
        target = (y, a * 4 + b * 2 + r, x, c, z)
        routes.append(
            (int(np.ravel_multi_index((x, zl, y, a, b), SIZES)), int(np.ravel_multi_index(target, SIZES)))
        )
    return routes


def local(queries, keys, values, out_weight, q_gain, k_gain, gate, valid_count):
    rows, width = queries.shape
    features = width * 16
    gathered = lax.all_gather(
        jnp.concatenate([keys, values], axis=1), "zl", axis=0, tiled=True, axis_index_groups=[RING]
    )
    weights = lax.ppermute(out_weight.T, AXES, weight_routes())

    squares = jnp.stack(
        [
            jnp.sum(jnp.square(queries.astype(F32)), axis=1),
            jnp.sum(jnp.square(keys.astype(F32)), axis=1),
        ]
    )
    near = lax.all_to_all(
        jnp.broadcast_to(squares[None], (8, 2, rows)), ("y", "core"), 0, 0, tiled=True
    )
    near = jnp.sum(near, axis=0)
    totals = near + lax.ppermute(near, "zh", SWAP)
    inverse = lax.rsqrt(totals / features + EPSILON)
    key_inverse = lax.all_to_all(
        jnp.broadcast_to(inverse[1][None], (8, rows)), "zl", 0, 0, tiled=True
    )
    key_inverse = jnp.concatenate([key_inverse[z] for z in RING])[None, :]
    query_norm = (queries.astype(F32) * inverse[0][:, None] * q_gain[None, :]).astype(BF16)
    query_all = lax.all_gather(query_norm, "x", axis=0, tiled=False)
    query_all, key_inverse, weights = lax.optimization_barrier((query_all, key_inverse, weights))
    weights = lax.all_gather(weights, "x", axis=0, tiled=False)
    weights = lax.all_gather(weights, "zl", axis=0, tiled=False, axis_index_groups=[RING])

    limit = valid_count[0] - lax.axis_index("x") * (8 * rows)
    starts = np.repeat(np.asarray(RING, np.int32) * rows, rows)
    position = jnp.asarray(starts + np.tile(np.arange(rows, dtype=np.int32), 8))
    bias = jnp.where(position < limit, 0.0, BIAS).astype(F32)[None, :]
    parts = attention(query_all, gathered, key_inverse, bias, k_gain[:, None])
    parts = lax.all_to_all(parts, "x", 0, 0, tiled=True)
    own = join(parts)
    across = lax.ppermute(own, "zh", SWAP)
    own_y = lax.all_gather(own, "y", axis=0, tiled=False)
    beside_y = lax.ppermute(own_y, "core", SWAP)
    across_y = lax.all_gather(across, "y", axis=0, tiled=False)
    both_y = lax.ppermute(across_y, "core", SWAP)
    place = jnp.stack([lax.axis_index("core"), lax.axis_index("zh")]).astype(jnp.int32)
    return project(place, (own_y, beside_y, across_y, both_y), weights, gate[None, :])


def solution(mesh):
    fine = Mesh(mesh.devices.reshape(SIZES), AXES)
    tokens, features = ("x", "zl"), ("y", "core", "zh")
    placed = (
        P(tokens, features),
        P(tokens, features),
        P(tokens, features),
        P(features, tokens),
        P(features),
        P(features),
        P(features),
        P(),
    )
    return jax.shard_map(
        local, mesh=fine, in_specs=placed, out_specs=P(tokens, features), check_vma=False
    )
```

```python
import functools
import math

import jax
import jax.numpy as jnp
import numpy as np
from jax import lax
from jax.experimental import pallas as pl
from jax.experimental.pallas import tpu as pltpu
from jax.sharding import Mesh
from jax.sharding import PartitionSpec as P

HEAD_DIM = 128
EPSILON = 1e-06
BIAS = -1e30
F32 = jnp.float32
BF16 = jnp.bfloat16
AXES = ("xh", "xl", "zl", "y", "core", "zh")
SIZES = (2, 2, 8, 4, 2, 2)
X = ("xh", "xl")
SWAP = ((0, 1), (1, 0))
RING = [0, 2, 4, 6, 7, 5, 3, 1]
LINES = 32


def attention_kernel(
    q_ref, kv_ref, inverse_ref, bias_ref, gain_ref, out_ref, kt_ref, ve_ref
):
    factor = HEAD_DIM**-0.5 * math.log2(math.e)
    blocks, rows, _ = q_ref.shape
    keys = kv_ref.shape[0]
    row = lax.broadcasted_iota(jnp.int32, (HEAD_DIM, keys), 0)
    bias = jnp.where(row == 0, bias_ref[...], 0.0).astype(BF16)
    for h in range(2):
        columns = slice(h * HEAD_DIM, (h + 1) * HEAD_DIM)
        raw = kv_ref[:, columns].T.astype(F32)
        kt_ref[h, :HEAD_DIM, :] = (raw * inverse_ref[...] * gain_ref[columns, :]).astype(BF16)
        kt_ref[h, HEAD_DIM:, :] = bias
        ve_ref[h, :, :HEAD_DIM] = kv_ref[:, (2 + h) * HEAD_DIM : (3 + h) * HEAD_DIM]
        ve_ref[h, :, HEAD_DIM:] = jnp.ones((keys, HEAD_DIM), BF16)

    lane = lax.broadcasted_iota(jnp.int32, (rows, HEAD_DIM), 1)
    first = jnp.where(lane == 0, 1.0, 0.0).astype(BF16)
    for i in range(blocks // 2):
        stats = [jnp.zeros((rows, HEAD_DIM), F32) for _ in range(2)]
        for j in range(2):
            scores = []
            for h in range(2):
                query = jnp.concatenate(
                    [q_ref[2 * i + j, :, h * HEAD_DIM : (h + 1) * HEAD_DIM], first], axis=1
                )
                scores.append(jnp.dot(query, kt_ref[h], preferred_element_type=F32))
            for h in range(2):
                top = (jnp.max(scores[h], axis=1, keepdims=True) * factor).astype(BF16).astype(F32)
                weights = jnp.exp2(scores[h] * factor - top).astype(BF16)
                summed = jnp.dot(weights, ve_ref[h], preferred_element_type=F32)
                out_ref[2 * i + h, j * rows : (j + 1) * rows, :] = summed[:, :HEAD_DIM].astype(BF16)
                mass = summed[:, HEAD_DIM:]
                high = mass.astype(BF16).astype(F32)
                stats[h] = jnp.where(lane == 3 * j, top, stats[h])
                stats[h] = jnp.where(lane == 3 * j + 1, high, stats[h])
                stats[h] = jnp.where(lane == 3 * j + 2, mass - high, stats[h])
        for h in range(2):
            lines = stats[h].T[:8]
            full = rows // HEAD_DIM
            pieces = [lines[:, n * HEAD_DIM : (n + 1) * HEAD_DIM] for n in range(full)]
            rest = lines[:, full * HEAD_DIM :]
            pieces.append(jnp.pad(rest, ((0, 0), (0, (full + 1) * HEAD_DIM - rows))))
            pieces += [jnp.zeros((8, HEAD_DIM), F32)] * (LINES // 8 - len(pieces))
            out_ref[2 * i + h, 2 * rows :, :] = jnp.concatenate(pieces).astype(BF16)


def attention(queries, keys_values, inverse, bias, gain):
    blocks, rows, width = queries.shape
    keys = keys_values.shape[0]
    shape = (blocks, 2 * rows + LINES, HEAD_DIM)
    return pl.pallas_call(
        attention_kernel,
        grid=(1,),
        in_specs=[
            pl.BlockSpec((blocks, rows, width), lambda i: (0, 0, 0)),
            pl.BlockSpec((keys, 2 * width), lambda i: (0, 0)),
            pl.BlockSpec((1, keys), lambda i: (0, 0)),
            pl.BlockSpec((1, keys), lambda i: (0, 0)),
            pl.BlockSpec((width, 1), lambda i: (0, 0)),
        ],
        out_specs=pl.BlockSpec(shape, lambda i: (0, 0, 0)),
        out_shape=jax.ShapeDtypeStruct(shape, BF16),
        scratch_shapes=[
            pltpu.VMEM((2, 2 * HEAD_DIM, keys), BF16),
            pltpu.VMEM((2, keys, 2 * HEAD_DIM), BF16),
        ],
        compiler_params=pltpu.CompilerParams(vmem_limit_bytes=48 << 20),
        cost_estimate=pl.CostEstimate(
            flops=8 * blocks * rows * keys * width,
            bytes_accessed=4 << 20,
            transcendentals=2 * blocks * rows * keys,
        ),
    )(queries, keys_values, inverse, bias, gain)


def join_kernel(parts_ref, out_ref):
    count = parts_ref.shape[0]
    rows = out_ref.shape[0] // 2
    lines = []
    for i in range(count):
        packed = parts_ref[i, 2 * rows :, :].astype(F32)
        lines.append(jnp.concatenate([packed[8 * n : 8 * n + 8] for n in range(LINES // 8)], axis=1))
    shares = []
    for j in range(2):
        tops = [line[3 * j : 3 * j + 1] for line in lines]
        highest = functools.reduce(jnp.maximum, tops)
        weights = [jnp.exp2(top - highest) for top in tops]
        mass = sum(
            w * (line[3 * j + 1 : 3 * j + 2] + line[3 * j + 2 : 3 * j + 3])
            for w, line in zip(weights, lines)
        )
        mass = jnp.where(mass == 0.0, 1.0, mass)
        shares += [w / mass for w in weights]
    spread = jnp.zeros((HEAD_DIM - 2 * count, lines[0].shape[1]), F32)
    columns = jnp.concatenate(shares + [spread]).T
    for j in range(2):
        span = slice(j * rows, (j + 1) * rows)
        total = jnp.zeros((rows, HEAD_DIM), F32)
        for i in range(count):
            share = columns[:rows, j * count + i : j * count + i + 1]
            total = total + share * parts_ref[i, span, :].astype(F32)
        out_ref[span, :] = total.astype(BF16)


def join(parts):
    return pl.pallas_call(
        join_kernel,
        out_shape=jax.ShapeDtypeStruct((parts.shape[1] - LINES, HEAD_DIM), BF16),
        compiler_params=pltpu.CompilerParams(vmem_limit_bytes=32 << 20),
    )(parts)


def project_kernel(
    place_ref, own_ref, core_ref, zh_ref, both_ref, weight_ref, kept_ref, sent_ref, total_ref
):
    core, zh, half = place_ref[0], place_ref[1], place_ref[2]
    step = pl.program_id(0)
    rows = kept_ref.shape[0]
    pieces, blocks = [], []
    for ref, a, b in (
        (own_ref, core, zh),
        (core_ref, 1 - core, zh),
        (zh_ref, core, 1 - zh),
        (both_ref, 1 - core, 1 - zh),
    ):
        pair = a * 2 + b
        pieces.append(ref[0])
        blocks.append(jnp.concatenate([weight_ref[pair, 0], weight_ref[7 - pair, 0]]))
    total = lax.dot_general(
        jnp.concatenate(pieces, axis=1),
        jnp.concatenate(blocks, axis=1),
        (((1,), (1,)), ((), ())),
        preferred_element_type=F32,
    )

    @pl.when(step == 0)
    def _():
        total_ref[...] = total

    @pl.when(step > 0)
    def _():
        total_ref[...] += total

    @pl.when(step == pl.num_programs(0) - 1)
    def _():
        kept_ref[...] = total_ref[pl.ds(pl.multiple_of(half * rows, 16), rows), :]
        sent_ref[...] = total_ref[pl.ds(pl.multiple_of((1 - half) * rows, 16), rows), :].astype(BF16)


def project(place, pieces, weights):
    groups, rows, width = pieces[0].shape
    blocks, _, columns, _ = weights.shape
    shape = (rows // 2, 2 * columns)
    return pl.pallas_call(
        project_kernel,
        grid=(groups,),
        in_specs=[pl.BlockSpec(memory_space=pltpu.SMEM)]
        + [pl.BlockSpec((1, rows, width), lambda i: (i, 0, 0))] * 4
        + [pl.BlockSpec((blocks, 1, columns, width), lambda i: (0, i, 0, 0))],
        out_specs=[pl.BlockSpec(shape, lambda i: (0, 0))] * 2,
        out_shape=[jax.ShapeDtypeStruct(shape, F32), jax.ShapeDtypeStruct(shape, BF16)],
        scratch_shapes=[pltpu.VMEM((rows, 2 * columns), F32)],
        compiler_params=pltpu.CompilerParams(vmem_limit_bytes=32 << 20),
    )(place, *pieces, weights)


def weight_routes():
    routes = []
    sizes = (4, 8, 4, 2, 2)
    for x, zl, y, a, b in np.ndindex(*sizes):
        c, z, r = zl // 4, zl // 2 % 2, zl % 2
        target = (y, a * 4 + b * 2 + r, x, c, z)
        routes.append(
            (int(np.ravel_multi_index((x, zl, y, a, b), sizes)), int(np.ravel_multi_index(target, sizes)))
        )
    return routes


def local(queries, keys, values, out_weight, q_gain, k_gain, gate, valid_count):
    rows, width = queries.shape
    features = width * 16
    gathered = lax.all_gather(
        jnp.concatenate([keys, values], axis=1), "zl", axis=0, tiled=True, axis_index_groups=[RING]
    )
    weights = lax.ppermute(out_weight.T, AXES, weight_routes())

    squares = jnp.stack(
        [
            jnp.sum(jnp.square(queries.astype(F32)), axis=1),
            jnp.sum(jnp.square(keys.astype(F32)), axis=1),
        ]
    )
    near = lax.all_to_all(
        jnp.broadcast_to(squares[None], (8, 2, rows)), ("y", "core"), 0, 0, tiled=True
    )
    near = jnp.sum(near, axis=0)
    totals = near + lax.ppermute(near, "zh", SWAP)
    inverse = lax.rsqrt(totals / features + EPSILON)
    key_inverse = lax.all_to_all(
        jnp.broadcast_to(inverse[1][None], (8, rows)), "zl", 0, 0, tiled=True
    )
    key_inverse = jnp.concatenate([key_inverse[z] for z in RING])[None, :]
    query_norm = (queries.astype(F32) * inverse[0][:, None] * q_gain[None, :]).astype(BF16)
    query_all = lax.all_gather(query_norm, X, axis=0, tiled=False)
    query_all, key_inverse, weights = lax.optimization_barrier((query_all, key_inverse, weights))
    halves = [weights[:, :HEAD_DIM], weights[:, HEAD_DIM:]]
    weights = lax.all_to_all(jnp.stack(halves + halves), X, 0, 0, tiled=True)
    weights = lax.all_gather(weights, "zl", axis=0, tiled=False, axis_index_groups=[RING])

    place_x = lax.axis_index("xh") * 2 + lax.axis_index("xl")
    limit = valid_count[0] - place_x * (8 * rows)
    starts = np.repeat(np.asarray(RING, np.int32) * rows, rows)
    position = jnp.asarray(starts + np.tile(np.arange(rows, dtype=np.int32), 8))
    bias = jnp.where(position < limit, 0.0, BIAS).astype(F32)[None, :]
    parts = attention(query_all, gathered, key_inverse, bias, k_gain[:, None])
    parts = lax.all_to_all(parts, X, 0, 0, tiled=True)
    own = join(parts)
    across = lax.ppermute(own, "zh", SWAP)
    own_y = lax.all_gather(own, "y", axis=0, tiled=False)
    beside_y = lax.ppermute(own_y, "core", SWAP)
    across_y = lax.all_gather(across, "y", axis=0, tiled=False)
    both_y = lax.ppermute(across_y, "core", SWAP)
    place = jnp.stack([lax.axis_index(n) for n in ("core", "zh", "xl")]).astype(jnp.int32)
    kept, sent = project(place, (own_y, beside_y, across_y, both_y), weights)
    summed = kept + lax.ppermute(sent, "xl", SWAP).astype(F32)
    return (gate[None, :] * summed).astype(BF16)


def solution(mesh):
    fine = Mesh(mesh.devices.reshape(SIZES), AXES)
    tokens, features = ("xh", "xl", "zl"), ("y", "core", "zh")
    placed = (
        P(tokens, features),
        P(tokens, features),
        P(tokens, features),
        P(features, tokens),
        P(features),
        P(features),
        P(features),
        P(),
    )
    return jax.shard_map(
        local, mesh=fine, in_specs=placed, out_specs=P(tokens, features), check_vma=False
    )
```

```python
import functools
import math

import jax
import jax.numpy as jnp
import numpy as np
from jax import lax
from jax.experimental import pallas as pl
from jax.experimental.pallas import tpu as pltpu
from jax.sharding import Mesh
from jax.sharding import PartitionSpec as P

HEAD_DIM = 128
EPSILON = 1e-06
BIAS = -1e30
F32 = jnp.float32
BF16 = jnp.bfloat16
AXES = ("x", "zl", "y", "core", "zh")
SIZES = (4, 8, 4, 2, 2)
SWAP = ((0, 1), (1, 0))
RING = [0, 2, 4, 6, 7, 5, 3, 1]
LATE = 112


def attention_kernel(
    q_ref, kv_ref, inverse_ref, bias_ref, gain_ref, out_ref, kt_ref, ve_ref
):
    factor = HEAD_DIM**-0.5 * math.log2(math.e)
    blocks, rows, width = q_ref.shape
    keys = kv_ref.shape[0]
    row = lax.broadcasted_iota(jnp.int32, (HEAD_DIM, keys), 0)
    bias = jnp.where(row == 0, bias_ref[...], 0.0).astype(BF16)
    for h in range(2):
        columns = slice(h * HEAD_DIM, (h + 1) * HEAD_DIM)
        raw = kv_ref[:, columns].T.astype(F32)
        kt_ref[h, :HEAD_DIM, :] = (raw * inverse_ref[...] * gain_ref[columns, :]).astype(BF16)
        kt_ref[h, HEAD_DIM:, :] = bias
        ve_ref[h, :, :HEAD_DIM] = kv_ref[:, (2 + h) * HEAD_DIM : (3 + h) * HEAD_DIM]
        ve_ref[h, :, HEAD_DIM:] = jnp.ones((keys, HEAD_DIM), BF16)

    lane = lax.broadcasted_iota(jnp.int32, (rows, HEAD_DIM), 1)
    first = jnp.where(lane == 0, 1.0, 0.0).astype(BF16)
    for b in range(blocks):
        stats = jnp.zeros((rows, HEAD_DIM), F32)
        scores = []
        for h in range(2):
            query = jnp.concatenate([q_ref[b, :, h * HEAD_DIM : (h + 1) * HEAD_DIM], first], axis=1)
            scores.append(jnp.dot(query, kt_ref[h], preferred_element_type=F32))
        for h in range(2):
            top = (jnp.max(scores[h], axis=1, keepdims=True) * factor).astype(BF16).astype(F32)
            weights = jnp.exp2(scores[h] * factor - top).astype(BF16)
            summed = jnp.dot(weights, ve_ref[h], preferred_element_type=F32)
            out_ref[b, :rows, h * HEAD_DIM : (h + 1) * HEAD_DIM] = summed[:, :HEAD_DIM].astype(BF16)
            mass = summed[:, HEAD_DIM:]
            high = mass.astype(BF16).astype(F32)
            stats = jnp.where(lane == 3 * h, top, stats)
            stats = jnp.where(lane == 3 * h + 1, high, stats)
            stats = jnp.where(lane == 3 * h + 2, mass - high, stats)
        lines = stats.T[:8]
        rest = jnp.pad(lines[:, width:], ((0, 0), (0, 2 * width - rows)))
        out_ref[b, rows:, :] = jnp.concatenate([lines[:, :width], rest]).astype(BF16)


def attention(queries, keys_values, inverse, bias, gain):
    blocks, rows, width = queries.shape
    keys = keys_values.shape[0]
    return pl.pallas_call(
        attention_kernel,
        grid=(1,),
        in_specs=[
            pl.BlockSpec((blocks, rows, width), lambda i: (0, 0, 0)),
            pl.BlockSpec((keys, 2 * width), lambda i: (0, 0)),
            pl.BlockSpec((1, keys), lambda i: (0, 0)),
            pl.BlockSpec((1, keys), lambda i: (0, 0)),
            pl.BlockSpec((width, 1), lambda i: (0, 0)),
        ],
        out_specs=pl.BlockSpec((blocks, rows + 16, width), lambda i: (0, 0, 0)),
        out_shape=jax.ShapeDtypeStruct((blocks, rows + 16, width), BF16),
        scratch_shapes=[
            pltpu.VMEM((2, 2 * HEAD_DIM, keys), BF16),
            pltpu.VMEM((2, keys, 2 * HEAD_DIM), BF16),
        ],
        compiler_params=pltpu.CompilerParams(vmem_limit_bytes=48 << 20),
        cost_estimate=pl.CostEstimate(
            flops=8 * blocks * rows * keys * width,
            bytes_accessed=4 << 20,
            transcendentals=2 * blocks * rows * keys,
        ),
    )(queries, keys_values, inverse, bias, gain)


def join_kernel(parts_ref, out_ref):
    count = parts_ref.shape[0]
    rows = out_ref.shape[0]
    lines = []
    for i in range(count):
        packed = parts_ref[i, rows:, :].astype(F32)
        lines.append(jnp.concatenate([packed[:8, :], packed[8:, :128]], axis=1))
    shares = []
    for h in range(2):
        tops = [line[3 * h : 3 * h + 1] for line in lines]
        highest = functools.reduce(jnp.maximum, tops)
        weights = [jnp.exp2(top - highest) for top in tops]
        mass = sum(
            w * (line[3 * h + 1 : 3 * h + 2] + line[3 * h + 2 : 3 * h + 3])
            for w, line in zip(weights, lines)
        )
        mass = jnp.where(mass == 0.0, 1.0, mass)
        shares += [w / mass for w in weights]
    spread = jnp.zeros((HEAD_DIM - 2 * count, lines[0].shape[1]), F32)
    columns = jnp.concatenate(shares + [spread]).T
    for h in range(2):
        span = slice(h * HEAD_DIM, (h + 1) * HEAD_DIM)
        total = jnp.zeros((rows, HEAD_DIM), F32)
        for i in range(count):
            share = columns[:rows, h * count + i : h * count + i + 1]
            total = total + share * parts_ref[i, :rows, span].astype(F32)
        out_ref[:, span] = total.astype(BF16)


def join(parts):
    return pl.pallas_call(
        join_kernel,
        out_shape=jax.ShapeDtypeStruct((parts.shape[1] - 16, parts.shape[2]), BF16),
        compiler_params=pltpu.CompilerParams(vmem_limit_bytes=32 << 20),
    )(parts)


def project_kernel(
    place_ref, own_ref, core_ref, zh_ref, both_ref, late_ref, early_ref, gate_ref, out_ref, total_ref
):
    core, zh = place_ref[0], place_ref[1]
    step = pl.program_id(0)
    few = out_ref.shape[1] // 2 - LATE
    pieces, blocks = [], []
    for ref, a, b in (
        (own_ref, core, zh),
        (core_ref, 1 - core, zh),
        (zh_ref, core, 1 - zh),
        (both_ref, 1 - core, 1 - zh),
    ):
        pair = a * 2 + b
        pieces.append(ref[0])
        block = []
        for r in range(2):
            start = pl.multiple_of(LATE + (2 * pair + r) * few, 16)
            block += [
                late_ref[pair if r == 0 else 7 - pair, 0],
                early_ref[0, pl.ds(start, few), :],
            ]
        blocks.append(jnp.concatenate(block))
    total = lax.dot_general(
        jnp.concatenate(pieces, axis=1),
        jnp.concatenate(blocks, axis=1),
        (((1,), (1,)), ((), ())),
        preferred_element_type=F32,
    )

    @pl.when(step == 0)
    def _():
        total_ref[...] = total

    @pl.when(step > 0)
    def _():
        total_ref[...] += total

    @pl.when(step == pl.num_programs(0) - 1)
    def _():
        out_ref[...] = (total_ref[...] * gate_ref[...]).astype(BF16)


def project(place, pieces, late, early, gate):
    groups, rows, width = pieces[0].shape
    shape = (rows, gate.shape[1])
    return pl.pallas_call(
        project_kernel,
        grid=(groups,),
        in_specs=[pl.BlockSpec(memory_space=pltpu.SMEM)]
        + [pl.BlockSpec((1, rows, width), lambda i: (i, 0, 0))] * 4
        + [
            pl.BlockSpec((late.shape[0], 1) + late.shape[2:], lambda i: (0, i, 0, 0)),
            pl.BlockSpec((1,) + early.shape[1:], lambda i: (i, 0, 0)),
            pl.BlockSpec((1, gate.shape[1]), lambda i: (0, 0)),
        ],
        out_specs=pl.BlockSpec(shape, lambda i: (0, 0)),
        out_shape=jax.ShapeDtypeStruct(shape, BF16),
        scratch_shapes=[pltpu.VMEM(shape, F32)],
        compiler_params=pltpu.CompilerParams(vmem_limit_bytes=32 << 20),
    )(place, *pieces, late, early, gate)


def weight_routes():
    routes = []
    for x, zl, y, a, b in np.ndindex(*SIZES):
        c, z, r = zl // 4, zl // 2 % 2, zl % 2
        target = (y, a * 4 + b * 2 + r, x, c, z)
        routes.append(
            (int(np.ravel_multi_index((x, zl, y, a, b), SIZES)), int(np.ravel_multi_index(target, SIZES)))
        )
    return routes


def local(queries, keys, values, out_weight, q_gain, k_gain, gate, valid_count):
    rows, width = queries.shape
    features = width * 16
    gathered = lax.all_gather(
        jnp.concatenate([keys, values], axis=1), "zl", axis=0, tiled=True, axis_index_groups=[RING]
    )
    weights = lax.ppermute(out_weight.T, AXES, weight_routes())

    squares = jnp.stack(
        [
            jnp.sum(jnp.square(queries.astype(F32)), axis=1),
            jnp.sum(jnp.square(keys.astype(F32)), axis=1),
        ]
    )
    near = lax.all_to_all(
        jnp.broadcast_to(squares[None], (8, 2, rows)), ("y", "core"), 0, 0, tiled=True
    )
    near = jnp.sum(near, axis=0)
    totals = near + lax.ppermute(near, "zh", SWAP)
    inverse = lax.rsqrt(totals / features + EPSILON)
    key_inverse = lax.all_to_all(
        jnp.broadcast_to(inverse[1][None], (8, rows)), "zl", 0, 0, tiled=True
    )
    key_inverse = jnp.concatenate([key_inverse[z] for z in RING])[None, :]
    query_norm = (queries.astype(F32) * inverse[0][:, None] * q_gain[None, :]).astype(BF16)
    query_all = lax.all_gather(query_norm, "x", axis=0, tiled=False)
    columns = out_weight.shape[1]
    early = lax.all_to_all(
        jnp.broadcast_to(weights[None, LATE:], (8, columns - LATE, width)), "zl", 0, 0, tiled=True
    )
    query_all, key_inverse, early = lax.optimization_barrier((query_all, key_inverse, early))
    along_x = lax.all_gather(
        jnp.concatenate([weights[:LATE], early.reshape(-1, width)]), "x", axis=0, tiled=False
    )
    late = lax.all_gather(
        along_x[:, :LATE], "zl", axis=0, tiled=False, axis_index_groups=[RING]
    )

    limit = valid_count[0] - lax.axis_index("x") * (8 * rows)
    starts = np.repeat(np.asarray(RING, np.int32) * rows, rows)
    position = jnp.asarray(starts + np.tile(np.arange(rows, dtype=np.int32), 8))
    bias = jnp.where(position < limit, 0.0, BIAS).astype(F32)[None, :]
    parts = attention(query_all, gathered, key_inverse, bias, k_gain[:, None])
    parts = lax.all_to_all(parts, "x", 0, 0, tiled=True)
    own = join(parts)
    across = lax.ppermute(own, "zh", SWAP)
    own_y = lax.all_gather(own, "y", axis=0, tiled=False)
    beside_y = lax.ppermute(own_y, "core", SWAP)
    across_y = lax.all_gather(across, "y", axis=0, tiled=False)
    both_y = lax.ppermute(across_y, "core", SWAP)
    place = jnp.stack([lax.axis_index("core"), lax.axis_index("zh")]).astype(jnp.int32)
    return project(place, (own_y, beside_y, across_y, both_y), late, along_x, gate[None, :])


def solution(mesh):
    fine = Mesh(mesh.devices.reshape(SIZES), AXES)
    tokens, features = ("x", "zl"), ("y", "core", "zh")
    placed = (
        P(tokens, features),
        P(tokens, features),
        P(tokens, features),
        P(features, tokens),
        P(features),
        P(features),
        P(features),
        P(),
    )
    return jax.shard_map(
        local, mesh=fine, in_specs=placed, out_specs=P(tokens, features), check_vma=False
    )
```

```python
import functools
import math

import jax
import jax.numpy as jnp
import numpy as np
from jax import lax
from jax.experimental import pallas as pl
from jax.experimental.pallas import tpu as pltpu
from jax.sharding import Mesh
from jax.sharding import PartitionSpec as P

HEAD_DIM = 128
EPSILON = 1e-06
BIAS = -1e30
F32 = jnp.float32
BF16 = jnp.bfloat16
AXES = ("x", "zl", "y", "core", "zh")
SIZES = (4, 8, 4, 2, 2)
SWAP = ((0, 1), (1, 0))
RING = [0, 2, 4, 6, 7, 5, 3, 1]
LATE = 128


def attention_kernel(
    q_ref, kv_ref, inverse_ref, bias_ref, gain_ref, out_ref, kt_ref, ve_ref
):
    factor = HEAD_DIM**-0.5 * math.log2(math.e)
    blocks, rows, width = q_ref.shape
    keys = kv_ref.shape[0]
    row = lax.broadcasted_iota(jnp.int32, (HEAD_DIM, keys), 0)
    bias = jnp.where(row == 0, bias_ref[...], 0.0).astype(BF16)
    for h in range(2):
        columns = slice(h * HEAD_DIM, (h + 1) * HEAD_DIM)
        raw = kv_ref[:, columns].T.astype(F32)
        kt_ref[h, :HEAD_DIM, :] = (raw * inverse_ref[...] * gain_ref[columns, :]).astype(BF16)
        kt_ref[h, HEAD_DIM:, :] = bias
        ve_ref[h, :, :HEAD_DIM] = kv_ref[:, (2 + h) * HEAD_DIM : (3 + h) * HEAD_DIM]
        ve_ref[h, :, HEAD_DIM:] = jnp.ones((keys, HEAD_DIM), BF16)

    lane = lax.broadcasted_iota(jnp.int32, (rows, HEAD_DIM), 1)
    first = jnp.where(lane == 0, 1.0, 0.0).astype(BF16)
    for b in range(blocks):
        stats = jnp.zeros((rows, HEAD_DIM), F32)
        scores = []
        for h in range(2):
            query = jnp.concatenate([q_ref[b, :, h * HEAD_DIM : (h + 1) * HEAD_DIM], first], axis=1)
            scores.append(jnp.dot(query, kt_ref[h], preferred_element_type=F32))
        for h in range(2):
            top = (jnp.max(scores[h], axis=1, keepdims=True) * factor).astype(BF16).astype(F32)
            weights = jnp.exp2(scores[h] * factor - top).astype(BF16)
            summed = jnp.dot(weights, ve_ref[h], preferred_element_type=F32)
            out_ref[b, :rows, h * HEAD_DIM : (h + 1) * HEAD_DIM] = summed[:, :HEAD_DIM].astype(BF16)
            mass = summed[:, HEAD_DIM:]
            high = mass.astype(BF16).astype(F32)
            stats = jnp.where(lane == 3 * h, top, stats)
            stats = jnp.where(lane == 3 * h + 1, high, stats)
            stats = jnp.where(lane == 3 * h + 2, mass - high, stats)
        lines = stats.T[:8]
        rest = jnp.pad(lines[:, width:], ((0, 0), (0, 2 * width - rows)))
        out_ref[b, rows:, :] = jnp.concatenate([lines[:, :width], rest]).astype(BF16)


def attention(queries, keys_values, inverse, bias, gain):
    blocks, rows, width = queries.shape
    keys = keys_values.shape[0]
    return pl.pallas_call(
        attention_kernel,
        grid=(1,),
        in_specs=[
            pl.BlockSpec((blocks, rows, width), lambda i: (0, 0, 0)),
            pl.BlockSpec((keys, 2 * width), lambda i: (0, 0)),
            pl.BlockSpec((1, keys), lambda i: (0, 0)),
            pl.BlockSpec((1, keys), lambda i: (0, 0)),
            pl.BlockSpec((width, 1), lambda i: (0, 0)),
        ],
        out_specs=pl.BlockSpec((blocks, rows + 16, width), lambda i: (0, 0, 0)),
        out_shape=jax.ShapeDtypeStruct((blocks, rows + 16, width), BF16),
        scratch_shapes=[
            pltpu.VMEM((2, 2 * HEAD_DIM, keys), BF16),
            pltpu.VMEM((2, keys, 2 * HEAD_DIM), BF16),
        ],
        compiler_params=pltpu.CompilerParams(vmem_limit_bytes=48 << 20),
        cost_estimate=pl.CostEstimate(
            flops=8 * blocks * rows * keys * width,
            bytes_accessed=4 << 20,
            transcendentals=2 * blocks * rows * keys,
        ),
    )(queries, keys_values, inverse, bias, gain)


def join_kernel(parts_ref, out_ref):
    count = parts_ref.shape[0]
    rows = out_ref.shape[0]
    lines = []
    for i in range(count):
        packed = parts_ref[i, rows:, :].astype(F32)
        lines.append(jnp.concatenate([packed[:8, :], packed[8:, :128]], axis=1))
    shares = []
    for h in range(2):
        tops = [line[3 * h : 3 * h + 1] for line in lines]
        highest = functools.reduce(jnp.maximum, tops)
        weights = [jnp.exp2(top - highest) for top in tops]
        mass = sum(
            w * (line[3 * h + 1 : 3 * h + 2] + line[3 * h + 2 : 3 * h + 3])
            for w, line in zip(weights, lines)
        )
        mass = jnp.where(mass == 0.0, 1.0, mass)
        shares += [w / mass for w in weights]
    spread = jnp.zeros((HEAD_DIM - 2 * count, lines[0].shape[1]), F32)
    columns = jnp.concatenate(shares + [spread]).T
    for h in range(2):
        span = slice(h * HEAD_DIM, (h + 1) * HEAD_DIM)
        total = jnp.zeros((rows, HEAD_DIM), F32)
        for i in range(count):
            share = columns[:rows, h * count + i : h * count + i + 1]
            total = total + share * parts_ref[i, :rows, span].astype(F32)
        out_ref[:, span] = total.astype(BF16)


def join(parts):
    return pl.pallas_call(
        join_kernel,
        out_shape=jax.ShapeDtypeStruct((parts.shape[1] - 16, parts.shape[2]), BF16),
        compiler_params=pltpu.CompilerParams(vmem_limit_bytes=32 << 20),
    )(parts)


def project_kernel(
    place_ref, own_ref, core_ref, zh_ref, both_ref, late_ref, early_ref, gate_ref, out_ref, total_ref
):
    core, zh = place_ref[0], place_ref[1]
    step = pl.program_id(0)
    few = out_ref.shape[1] // 2 - LATE
    pieces, blocks = [], []
    for ref, a, b in (
        (own_ref, core, zh),
        (core_ref, 1 - core, zh),
        (zh_ref, core, 1 - zh),
        (both_ref, 1 - core, 1 - zh),
    ):
        pair = a * 2 + b
        pieces.append(ref[0])
        block = []
        for r in range(2):
            start = pl.multiple_of(LATE + (2 * pair + r) * few, 16)
            block += [
                late_ref[pair if r == 0 else 7 - pair, 0],
                early_ref[0, pl.ds(start, few), :],
            ]
        blocks.append(jnp.concatenate(block))
    total = lax.dot_general(
        jnp.concatenate(pieces, axis=1),
        jnp.concatenate(blocks, axis=1),
        (((1,), (1,)), ((), ())),
        preferred_element_type=F32,
    )

    @pl.when(step == 0)
    def _():
        total_ref[...] = total

    @pl.when(step > 0)
    def _():
        total_ref[...] += total

    @pl.when(step == pl.num_programs(0) - 1)
    def _():
        out_ref[...] = (total_ref[...] * gate_ref[...]).astype(BF16)


def project(place, pieces, late, early, gate):
    groups, rows, width = pieces[0].shape
    shape = (rows, gate.shape[1])
    return pl.pallas_call(
        project_kernel,
        grid=(groups,),
        in_specs=[pl.BlockSpec(memory_space=pltpu.SMEM)]
        + [pl.BlockSpec((1, rows, width), lambda i: (i, 0, 0))] * 4
        + [
            pl.BlockSpec((late.shape[0], 1) + late.shape[2:], lambda i: (0, i, 0, 0)),
            pl.BlockSpec((1,) + early.shape[1:], lambda i: (i, 0, 0)),
            pl.BlockSpec((1, gate.shape[1]), lambda i: (0, 0)),
        ],
        out_specs=pl.BlockSpec(shape, lambda i: (0, 0)),
        out_shape=jax.ShapeDtypeStruct(shape, BF16),
        scratch_shapes=[pltpu.VMEM(shape, F32)],
        compiler_params=pltpu.CompilerParams(vmem_limit_bytes=32 << 20),
    )(place, *pieces, late, early, gate)


def weight_routes():
    routes = []
    for x, zl, y, a, b in np.ndindex(*SIZES):
        c, z, r = zl // 4, zl // 2 % 2, zl % 2
        target = (y, a * 4 + b * 2 + r, x, c, z)
        routes.append(
            (int(np.ravel_multi_index((x, zl, y, a, b), SIZES)), int(np.ravel_multi_index(target, SIZES)))
        )
    return routes


def local(queries, keys, values, out_weight, q_gain, k_gain, gate, valid_count):
    rows, width = queries.shape
    features = width * 16
    gathered = lax.all_gather(
        jnp.concatenate([keys, values], axis=1), "zl", axis=0, tiled=True, axis_index_groups=[RING]
    )
    weights = lax.ppermute(out_weight.T, AXES, weight_routes())

    squares = jnp.stack(
        [
            jnp.sum(jnp.square(queries.astype(F32)), axis=1),
            jnp.sum(jnp.square(keys.astype(F32)), axis=1),
        ]
    )
    near = lax.all_to_all(
        jnp.broadcast_to(squares[None], (8, 2, rows)), ("y", "core"), 0, 0, tiled=True
    )
    near = jnp.sum(near, axis=0)
    totals = near + lax.ppermute(near, "zh", SWAP)
    inverse = lax.rsqrt(totals / features + EPSILON)
    key_inverse = lax.all_to_all(
        jnp.broadcast_to(inverse[1][None], (8, rows)), "zl", 0, 0, tiled=True
    )
    key_inverse = jnp.concatenate([key_inverse[z] for z in RING])[None, :]
    query_norm = (queries.astype(F32) * inverse[0][:, None] * q_gain[None, :]).astype(BF16)
    query_all = lax.all_gather(query_norm, "x", axis=0, tiled=False)
    columns = out_weight.shape[1]
    query_all, key_inverse, weights = lax.optimization_barrier((query_all, key_inverse, weights))
    early = lax.all_to_all(
        jnp.broadcast_to(weights[None, LATE:], (8, columns - LATE, width)), "zl", 0, 0, tiled=True
    )
    along_x = lax.all_gather(
        jnp.concatenate([weights[:LATE], early.reshape(-1, width)]), "x", axis=0, tiled=False
    )
    late = lax.all_gather(
        along_x[:, :LATE], "zl", axis=0, tiled=False, axis_index_groups=[RING]
    )

    limit = valid_count[0] - lax.axis_index("x") * (8 * rows)
    starts = np.repeat(np.asarray(RING, np.int32) * rows, rows)
    position = jnp.asarray(starts + np.tile(np.arange(rows, dtype=np.int32), 8))
    bias = jnp.where(position < limit, 0.0, BIAS).astype(F32)[None, :]
    parts = attention(query_all, gathered, key_inverse, bias, k_gain[:, None])
    parts = lax.all_to_all(parts, "x", 0, 0, tiled=True)
    own = join(parts)
    across = lax.ppermute(own, "zh", SWAP)
    own_y = lax.all_gather(own, "y", axis=0, tiled=False)
    beside_y = lax.ppermute(own_y, "core", SWAP)
    across_y = lax.all_gather(across, "y", axis=0, tiled=False)
    both_y = lax.ppermute(across_y, "core", SWAP)
    place = jnp.stack([lax.axis_index("core"), lax.axis_index("zh")]).astype(jnp.int32)
    return project(place, (own_y, beside_y, across_y, both_y), late, along_x, gate[None, :])


def solution(mesh):
    fine = Mesh(mesh.devices.reshape(SIZES), AXES)
    tokens, features = ("x", "zl"), ("y", "core", "zh")
    placed = (
        P(tokens, features),
        P(tokens, features),
        P(tokens, features),
        P(features, tokens),
        P(features),
        P(features),
        P(features),
        P(),
    )
    return jax.shard_map(
        local, mesh=fine, in_specs=placed, out_specs=P(tokens, features), check_vma=False
    )
```

```python
import functools
import math

import jax
import jax.numpy as jnp
import numpy as np
from jax import lax
from jax.experimental import pallas as pl
from jax.experimental.pallas import tpu as pltpu
from jax.sharding import Mesh
from jax.sharding import PartitionSpec as P

HEAD_DIM = 128
EPSILON = 1e-06
BIAS = -1e30
F32 = jnp.float32
BF16 = jnp.bfloat16
AXES = ("x", "zl", "y", "core", "zh")
SIZES = (4, 8, 4, 2, 2)
SWAP = ((0, 1), (1, 0))
RING = [0, 2, 4, 6, 7, 5, 3, 1]
LATE = 128


def attention_kernel(
    q_ref, kv_ref, inverse_ref, bias_ref, gain_ref, out_ref, kt_ref, ve_ref
):
    factor = HEAD_DIM**-0.5 * math.log2(math.e)
    blocks, rows, width = q_ref.shape
    keys = kv_ref.shape[0]
    row = lax.broadcasted_iota(jnp.int32, (HEAD_DIM, keys), 0)
    bias = jnp.where(row == 0, bias_ref[...], 0.0).astype(BF16)
    for h in range(2):
        columns = slice(h * HEAD_DIM, (h + 1) * HEAD_DIM)
        raw = kv_ref[:, columns].T.astype(F32)
        kt_ref[h, :HEAD_DIM, :] = (raw * inverse_ref[...] * gain_ref[columns, :]).astype(BF16)
        kt_ref[h, HEAD_DIM:, :] = bias
        ve_ref[h, :, :HEAD_DIM] = kv_ref[:, (2 + h) * HEAD_DIM : (3 + h) * HEAD_DIM]
        ve_ref[h, :, HEAD_DIM:] = jnp.ones((keys, HEAD_DIM), BF16)

    lane = lax.broadcasted_iota(jnp.int32, (rows, HEAD_DIM), 1)
    first = jnp.where(lane == 0, 1.0, 0.0).astype(BF16)
    for b in range(blocks):
        stats = jnp.zeros((rows, HEAD_DIM), F32)
        scores = []
        for h in range(2):
            query = jnp.concatenate([q_ref[b, :, h * HEAD_DIM : (h + 1) * HEAD_DIM], first], axis=1)
            scores.append(jnp.dot(query, kt_ref[h], preferred_element_type=F32))
        for h in range(2):
            top = (jnp.max(scores[h], axis=1, keepdims=True) * factor).astype(BF16).astype(F32)
            weights = jnp.exp2(scores[h] * factor - top).astype(BF16)
            summed = jnp.dot(weights, ve_ref[h], preferred_element_type=F32)
            out_ref[b, :rows, h * HEAD_DIM : (h + 1) * HEAD_DIM] = summed[:, :HEAD_DIM].astype(BF16)
            mass = summed[:, HEAD_DIM:]
            high = mass.astype(BF16).astype(F32)
            stats = jnp.where(lane == 3 * h, top, stats)
            stats = jnp.where(lane == 3 * h + 1, high, stats)
            stats = jnp.where(lane == 3 * h + 2, mass - high, stats)
        lines = stats.T[:8]
        rest = jnp.pad(lines[:, width:], ((0, 0), (0, 2 * width - rows)))
        out_ref[b, rows:, :] = jnp.concatenate([lines[:, :width], rest]).astype(BF16)


def attention(queries, keys_values, inverse, bias, gain):
    blocks, rows, width = queries.shape
    keys = keys_values.shape[0]
    return pl.pallas_call(
        attention_kernel,
        grid=(1,),
        in_specs=[
            pl.BlockSpec((blocks, rows, width), lambda i: (0, 0, 0)),
            pl.BlockSpec((keys, 2 * width), lambda i: (0, 0)),
            pl.BlockSpec((1, keys), lambda i: (0, 0)),
            pl.BlockSpec((1, keys), lambda i: (0, 0)),
            pl.BlockSpec((width, 1), lambda i: (0, 0)),
        ],
        out_specs=pl.BlockSpec((blocks, rows + 16, width), lambda i: (0, 0, 0)),
        out_shape=jax.ShapeDtypeStruct((blocks, rows + 16, width), BF16),
        scratch_shapes=[
            pltpu.VMEM((2, 2 * HEAD_DIM, keys), BF16),
            pltpu.VMEM((2, keys, 2 * HEAD_DIM), BF16),
        ],
        compiler_params=pltpu.CompilerParams(vmem_limit_bytes=48 << 20),
        cost_estimate=pl.CostEstimate(
            flops=8 * blocks * rows * keys * width,
            bytes_accessed=4 << 20,
            transcendentals=2 * blocks * rows * keys,
        ),
    )(queries, keys_values, inverse, bias, gain)


def join_kernel(parts_ref, out_ref):
    count = parts_ref.shape[0]
    rows = out_ref.shape[0]
    lines = []
    for i in range(count):
        packed = parts_ref[i, rows:, :].astype(F32)
        lines.append(jnp.concatenate([packed[:8, :], packed[8:, :128]], axis=1))
    shares = []
    for h in range(2):
        tops = [line[3 * h : 3 * h + 1] for line in lines]
        highest = functools.reduce(jnp.maximum, tops)
        weights = [jnp.exp2(top - highest) for top in tops]
        mass = sum(
            w * (line[3 * h + 1 : 3 * h + 2] + line[3 * h + 2 : 3 * h + 3])
            for w, line in zip(weights, lines)
        )
        mass = jnp.where(mass == 0.0, 1.0, mass)
        shares += [w / mass for w in weights]
    spread = jnp.zeros((HEAD_DIM - 2 * count, lines[0].shape[1]), F32)
    columns = jnp.concatenate(shares + [spread]).T
    for h in range(2):
        span = slice(h * HEAD_DIM, (h + 1) * HEAD_DIM)
        total = jnp.zeros((rows, HEAD_DIM), F32)
        for i in range(count):
            share = columns[:rows, h * count + i : h * count + i + 1]
            total = total + share * parts_ref[i, :rows, span].astype(F32)
        out_ref[:, span] = total.astype(BF16)


def join(parts):
    return pl.pallas_call(
        join_kernel,
        out_shape=jax.ShapeDtypeStruct((parts.shape[1] - 16, parts.shape[2]), BF16),
        compiler_params=pltpu.CompilerParams(vmem_limit_bytes=32 << 20),
    )(parts)


def project_kernel(
    place_ref, own_ref, core_ref, zh_ref, both_ref, late_ref, early_ref, gate_ref, out_ref, total_ref
):
    core, zh = place_ref[0], place_ref[1]
    step = pl.program_id(0)
    few = out_ref.shape[1] // 2 - LATE
    pieces, blocks = [], []
    for ref, a, b in (
        (own_ref, core, zh),
        (core_ref, 1 - core, zh),
        (zh_ref, core, 1 - zh),
        (both_ref, 1 - core, 1 - zh),
    ):
        pair = a * 2 + b
        pieces.append(ref[0])
        block = []
        for r in range(2):
            start = pl.multiple_of(LATE + (2 * pair + r) * few, 16)
            block += [
                late_ref[pair if r == 0 else 7 - pair, 0],
                early_ref[0, pl.ds(start, few), :],
            ]
        blocks.append(jnp.concatenate(block))
    total = lax.dot_general(
        jnp.concatenate(pieces, axis=1),
        jnp.concatenate(blocks, axis=1),
        (((1,), (1,)), ((), ())),
        preferred_element_type=F32,
    )

    @pl.when(step == 0)
    def _():
        total_ref[...] = total

    @pl.when(step > 0)
    def _():
        total_ref[...] += total

    @pl.when(step == pl.num_programs(0) - 1)
    def _():
        out_ref[...] = (total_ref[...] * gate_ref[...]).astype(BF16)


def project(place, pieces, late, early, gate):
    groups, rows, width = pieces[0].shape
    shape = (rows, gate.shape[1])
    return pl.pallas_call(
        project_kernel,
        grid=(groups,),
        in_specs=[pl.BlockSpec(memory_space=pltpu.SMEM)]
        + [pl.BlockSpec((1, rows, width), lambda i: (i, 0, 0))] * 4
        + [
            pl.BlockSpec((late.shape[0], 1) + late.shape[2:], lambda i: (0, i, 0, 0)),
            pl.BlockSpec((1,) + early.shape[1:], lambda i: (i, 0, 0)),
            pl.BlockSpec((1, gate.shape[1]), lambda i: (0, 0)),
        ],
        out_specs=pl.BlockSpec(shape, lambda i: (0, 0)),
        out_shape=jax.ShapeDtypeStruct(shape, BF16),
        scratch_shapes=[pltpu.VMEM(shape, F32)],
        compiler_params=pltpu.CompilerParams(vmem_limit_bytes=32 << 20),
    )(place, *pieces, late, early, gate)


def weight_routes():
    routes = []
    for x, zl, y, a, b in np.ndindex(*SIZES):
        c, z, r = zl // 4, zl // 2 % 2, zl % 2
        target = (y, a * 4 + b * 2 + r, x, c, z)
        routes.append(
            (int(np.ravel_multi_index((x, zl, y, a, b), SIZES)), int(np.ravel_multi_index(target, SIZES)))
        )
    return routes


def local(queries, keys, values, out_weight, q_gain, k_gain, gate, valid_count):
    rows, width = queries.shape
    features = width * 16
    gathered = lax.all_gather(
        jnp.concatenate([keys, values], axis=1), "zl", axis=0, tiled=True, axis_index_groups=[RING]
    )
    weights = lax.ppermute(out_weight.T, AXES, weight_routes())

    squares = jnp.stack(
        [
            jnp.sum(jnp.square(queries.astype(F32)), axis=1),
            jnp.sum(jnp.square(keys.astype(F32)), axis=1),
        ]
    )
    near = lax.all_to_all(
        jnp.broadcast_to(squares[None], (8, 2, rows)), ("y", "core"), 0, 0, tiled=True
    )
    near = jnp.sum(near, axis=0)
    totals = near + lax.ppermute(near, "zh", SWAP)
    inverse = lax.rsqrt(totals / features + EPSILON)
    key_inverse = lax.all_to_all(
        jnp.broadcast_to(inverse[1][None], (8, rows)), "zl", 0, 0, tiled=True
    )
    key_inverse = jnp.concatenate([key_inverse[z] for z in RING])[None, :]
    query_norm = (queries.astype(F32) * inverse[0][:, None] * q_gain[None, :]).astype(BF16)
    query_all = lax.all_gather(query_norm, "x", axis=0, tiled=False)
    columns = out_weight.shape[1]
    early = lax.all_to_all(
        jnp.broadcast_to(weights[None, LATE:], (8, columns - LATE, width)), "zl", 0, 0, tiled=True
    )
    query_all, key_inverse, early = lax.optimization_barrier((query_all, key_inverse, early))
    along_x = lax.all_gather(
        jnp.concatenate([weights[:LATE], early.reshape(-1, width)]), "x", axis=0, tiled=False
    )
    late = lax.all_gather(
        along_x[:, :LATE], "zl", axis=0, tiled=False, axis_index_groups=[RING]
    )

    limit = valid_count[0] - lax.axis_index("x") * (8 * rows)
    starts = np.repeat(np.asarray(RING, np.int32) * rows, rows)
    position = jnp.asarray(starts + np.tile(np.arange(rows, dtype=np.int32), 8))
    bias = jnp.where(position < limit, 0.0, BIAS).astype(F32)[None, :]
    parts = attention(query_all, gathered, key_inverse, bias, k_gain[:, None])
    parts = lax.all_to_all(parts, "x", 0, 0, tiled=True)
    own = join(parts)
    across = lax.ppermute(own, "zh", SWAP)
    own_y = lax.all_gather(own, "y", axis=0, tiled=False)
    beside_y = lax.ppermute(own_y, "core", SWAP)
    across_y = lax.all_gather(across, "y", axis=0, tiled=False)
    both_y = lax.ppermute(across_y, "core", SWAP)
    place = jnp.stack([lax.axis_index("core"), lax.axis_index("zh")]).astype(jnp.int32)
    return project(place, (own_y, beside_y, across_y, both_y), late, along_x, gate[None, :])


def solution(mesh):
    fine = Mesh(mesh.devices.reshape(SIZES), AXES)
    tokens, features = ("x", "zl"), ("y", "core", "zh")
    placed = (
        P(tokens, features),
        P(tokens, features),
        P(tokens, features),
        P(features, tokens),
        P(features),
        P(features),
        P(features),
        P(),
    )
    return jax.shard_map(
        local, mesh=fine, in_specs=placed, out_specs=P(tokens, features), check_vma=False
    )
```

```python
import functools
import math

import jax
import jax.numpy as jnp
import numpy as np
from jax import lax
from jax.experimental import pallas as pl
from jax.experimental.pallas import tpu as pltpu
from jax.sharding import Mesh
from jax.sharding import PartitionSpec as P

HEAD_DIM = 128
EPSILON = 1e-06
BIAS = -1e30
F32 = jnp.float32
BF16 = jnp.bfloat16
AXES = ("x", "zl", "y", "core", "zh")
SIZES = (4, 8, 4, 2, 2)
SWAP = ((0, 1), (1, 0))
RING = [0, 2, 4, 6, 7, 5, 3, 1]
LATE = 128


def attention_kernel(
    q_ref, kv_ref, inverse_ref, bias_ref, gain_ref, out_ref, kt_ref, ve_ref
):
    factor = HEAD_DIM**-0.5 * math.log2(math.e)
    blocks, rows, width = q_ref.shape
    keys = kv_ref.shape[0]
    row = lax.broadcasted_iota(jnp.int32, (HEAD_DIM, keys), 0)
    bias = jnp.where(row == 0, bias_ref[...], 0.0).astype(BF16)
    for h in range(2):
        columns = slice(h * HEAD_DIM, (h + 1) * HEAD_DIM)
        raw = kv_ref[:, columns].T.astype(F32)
        kt_ref[h, :HEAD_DIM, :] = (raw * inverse_ref[...] * gain_ref[columns, :]).astype(BF16)
        kt_ref[h, HEAD_DIM:, :] = bias
        ve_ref[h, :, :HEAD_DIM] = kv_ref[:, (2 + h) * HEAD_DIM : (3 + h) * HEAD_DIM]
        ve_ref[h, :, HEAD_DIM:] = jnp.ones((keys, HEAD_DIM), BF16)

    lane = lax.broadcasted_iota(jnp.int32, (rows, HEAD_DIM), 1)
    first = jnp.where(lane == 0, 1.0, 0.0).astype(BF16)
    for b in range(blocks):
        stats = jnp.zeros((rows, HEAD_DIM), F32)
        scores = []
        for h in range(2):
            query = jnp.concatenate([q_ref[b, :, h * HEAD_DIM : (h + 1) * HEAD_DIM], first], axis=1)
            scores.append(jnp.dot(query, kt_ref[h], preferred_element_type=F32))
        for h in range(2):
            top = (jnp.max(scores[h], axis=1, keepdims=True) * factor).astype(BF16).astype(F32)
            weights = jnp.exp2(scores[h] * factor - top).astype(BF16)
            summed = jnp.dot(weights, ve_ref[h], preferred_element_type=F32)
            out_ref[b, :rows, h * HEAD_DIM : (h + 1) * HEAD_DIM] = summed[:, :HEAD_DIM].astype(BF16)
            mass = summed[:, HEAD_DIM:]
            high = mass.astype(BF16).astype(F32)
            stats = jnp.where(lane == 3 * h, top, stats)
            stats = jnp.where(lane == 3 * h + 1, high, stats)
            stats = jnp.where(lane == 3 * h + 2, mass - high, stats)
        lines = stats.T[:8]
        rest = jnp.pad(lines[:, width:], ((0, 0), (0, 2 * width - rows)))
        out_ref[b, rows:, :] = jnp.concatenate([lines[:, :width], rest]).astype(BF16)


def attention(queries, keys_values, inverse, bias, gain):
    blocks, rows, width = queries.shape
    keys = keys_values.shape[0]
    return pl.pallas_call(
        attention_kernel,
        grid=(1,),
        in_specs=[
            pl.BlockSpec((blocks, rows, width), lambda i: (0, 0, 0)),
            pl.BlockSpec((keys, 2 * width), lambda i: (0, 0)),
            pl.BlockSpec((1, keys), lambda i: (0, 0)),
            pl.BlockSpec((1, keys), lambda i: (0, 0)),
            pl.BlockSpec((width, 1), lambda i: (0, 0)),
        ],
        out_specs=pl.BlockSpec((blocks, rows + 16, width), lambda i: (0, 0, 0)),
        out_shape=jax.ShapeDtypeStruct((blocks, rows + 16, width), BF16),
        scratch_shapes=[
            pltpu.VMEM((2, 2 * HEAD_DIM, keys), BF16),
            pltpu.VMEM((2, keys, 2 * HEAD_DIM), BF16),
        ],
        compiler_params=pltpu.CompilerParams(vmem_limit_bytes=48 << 20),
        cost_estimate=pl.CostEstimate(
            flops=8 * blocks * rows * keys * width,
            bytes_accessed=4 << 20,
            transcendentals=2 * blocks * rows * keys,
        ),
    )(queries, keys_values, inverse, bias, gain)


def join_kernel(parts_ref, out_ref):
    count = parts_ref.shape[0]
    rows = out_ref.shape[0]
    lines = []
    for i in range(count):
        packed = parts_ref[i, rows:, :].astype(F32)
        lines.append(jnp.concatenate([packed[:8, :], packed[8:, :128]], axis=1))
    shares = []
    for h in range(2):
        tops = [line[3 * h : 3 * h + 1] for line in lines]
        highest = functools.reduce(jnp.maximum, tops)
        weights = [jnp.exp2(top - highest) for top in tops]
        mass = sum(
            w * (line[3 * h + 1 : 3 * h + 2] + line[3 * h + 2 : 3 * h + 3])
            for w, line in zip(weights, lines)
        )
        mass = jnp.where(mass == 0.0, 1.0, mass)
        shares += [w / mass for w in weights]
    spread = jnp.zeros((HEAD_DIM - 2 * count, lines[0].shape[1]), F32)
    columns = jnp.concatenate(shares + [spread]).T
    for h in range(2):
        span = slice(h * HEAD_DIM, (h + 1) * HEAD_DIM)
        total = jnp.zeros((rows, HEAD_DIM), F32)
        for i in range(count):
            share = columns[:rows, h * count + i : h * count + i + 1]
            total = total + share * parts_ref[i, :rows, span].astype(F32)
        out_ref[:, span] = total.astype(BF16)


def join(parts):
    return pl.pallas_call(
        join_kernel,
        out_shape=jax.ShapeDtypeStruct((parts.shape[1] - 16, parts.shape[2]), BF16),
        compiler_params=pltpu.CompilerParams(vmem_limit_bytes=32 << 20),
    )(parts)


def project_kernel(
    place_ref, own_ref, core_ref, zh_ref, both_ref, late_ref, early_ref, gate_ref, out_ref, total_ref
):
    core, zh = place_ref[0], place_ref[1]
    step = pl.program_id(0)
    few = out_ref.shape[1] // 2 - LATE
    pieces, blocks = [], []
    for ref, a, b in (
        (own_ref, core, zh),
        (core_ref, 1 - core, zh),
        (zh_ref, core, 1 - zh),
        (both_ref, 1 - core, 1 - zh),
    ):
        pair = a * 2 + b
        pieces.append(ref[0])
        block = []
        for r in range(2):
            start = pl.multiple_of(LATE + (2 * pair + r) * few, 16)
            block += [
                late_ref[pair if r == 0 else 7 - pair, 0],
                early_ref[0, pl.ds(start, few), :],
            ]
        blocks.append(jnp.concatenate(block))
    total = lax.dot_general(
        jnp.concatenate(pieces, axis=1),
        jnp.concatenate(blocks, axis=1),
        (((1,), (1,)), ((), ())),
        preferred_element_type=F32,
    )

    @pl.when(step == 0)
    def _():
        total_ref[...] = total

    @pl.when(step > 0)
    def _():
        total_ref[...] += total

    @pl.when(step == pl.num_programs(0) - 1)
    def _():
        out_ref[...] = (total_ref[...] * gate_ref[...]).astype(BF16)


def project(place, pieces, late, early, gate):
    groups, rows, width = pieces[0].shape
    shape = (rows, gate.shape[1])
    return pl.pallas_call(
        project_kernel,
        grid=(groups,),
        in_specs=[pl.BlockSpec(memory_space=pltpu.SMEM)]
        + [pl.BlockSpec((1, rows, width), lambda i: (i, 0, 0))] * 4
        + [
            pl.BlockSpec((late.shape[0], 1) + late.shape[2:], lambda i: (0, i, 0, 0)),
            pl.BlockSpec((1,) + early.shape[1:], lambda i: (i, 0, 0)),
            pl.BlockSpec((1, gate.shape[1]), lambda i: (0, 0)),
        ],
        out_specs=pl.BlockSpec(shape, lambda i: (0, 0)),
        out_shape=jax.ShapeDtypeStruct(shape, BF16),
        scratch_shapes=[pltpu.VMEM(shape, F32)],
        compiler_params=pltpu.CompilerParams(vmem_limit_bytes=60 << 20),
    )(place, *pieces, late, early, gate)


def weight_routes():
    routes = []
    for x, zl, y, a, b in np.ndindex(*SIZES):
        c, z, r = zl // 4, zl // 2 % 2, zl % 2
        target = (y, a * 4 + b * 2 + r, x, c, z)
        routes.append(
            (int(np.ravel_multi_index((x, zl, y, a, b), SIZES)), int(np.ravel_multi_index(target, SIZES)))
        )
    return routes


def local(queries, keys, values, out_weight, q_gain, k_gain, gate, valid_count):
    rows, width = queries.shape
    features = width * 16
    gathered = lax.all_gather(
        jnp.concatenate([keys, values], axis=1), "zl", axis=0, tiled=True, axis_index_groups=[RING]
    )
    weights = lax.ppermute(out_weight.T, AXES, weight_routes())

    squares = jnp.stack(
        [
            jnp.sum(jnp.square(queries.astype(F32)), axis=1),
            jnp.sum(jnp.square(keys.astype(F32)), axis=1),
        ]
    )
    near = lax.all_to_all(
        jnp.broadcast_to(squares[None], (8, 2, rows)), ("y", "core"), 0, 0, tiled=True
    )
    near = jnp.sum(near, axis=0)
    totals = near + lax.ppermute(near, "zh", SWAP)
    inverse = lax.rsqrt(totals / features + EPSILON)
    key_inverse = lax.all_to_all(
        jnp.broadcast_to(inverse[1][None], (8, rows)), "zl", 0, 0, tiled=True
    )
    key_inverse = jnp.concatenate([key_inverse[z] for z in RING])[None, :]
    query_norm = (queries.astype(F32) * inverse[0][:, None] * q_gain[None, :]).astype(BF16)
    query_all = lax.all_gather(query_norm, "x", axis=0, tiled=False)
    columns = out_weight.shape[1]
    early = lax.all_to_all(
        jnp.broadcast_to(weights[None, LATE:], (8, columns - LATE, width)), "zl", 0, 0, tiled=True
    )
    query_all, key_inverse, early = lax.optimization_barrier((query_all, key_inverse, early))
    along_x = lax.all_gather(
        jnp.concatenate([weights[:LATE], early.reshape(-1, width)]), "x", axis=0, tiled=False
    )
    late = lax.all_gather(
        along_x[:, :LATE], "zl", axis=0, tiled=False, axis_index_groups=[RING]
    )

    limit = valid_count[0] - lax.axis_index("x") * (8 * rows)
    starts = np.repeat(np.asarray(RING, np.int32) * rows, rows)
    position = jnp.asarray(starts + np.tile(np.arange(rows, dtype=np.int32), 8))
    bias = jnp.where(position < limit, 0.0, BIAS).astype(F32)[None, :]
    parts = attention(query_all, gathered, key_inverse, bias, k_gain[:, None])
    parts = lax.all_to_all(parts, "x", 0, 0, tiled=True)
    own = join(parts)
    across = lax.ppermute(own, "zh", SWAP)
    own_y = lax.all_gather(own, "y", axis=0, tiled=False)
    beside_y = lax.ppermute(own_y, "core", SWAP)
    across_y = lax.all_gather(across, "y", axis=0, tiled=False)
    both_y = lax.ppermute(across_y, "core", SWAP)
    place = jnp.stack([lax.axis_index("core"), lax.axis_index("zh")]).astype(jnp.int32)
    return project(place, (own_y, beside_y, across_y, both_y), late, along_x, gate[None, :])


def solution(mesh):
    fine = Mesh(mesh.devices.reshape(SIZES), AXES)
    tokens, features = ("x", "zl"), ("y", "core", "zh")
    placed = (
        P(tokens, features),
        P(tokens, features),
        P(tokens, features),
        P(features, tokens),
        P(features),
        P(features),
        P(features),
        P(),
    )
    return jax.shard_map(
        local, mesh=fine, in_specs=placed, out_specs=P(tokens, features), check_vma=False
    )
```
